256 devices in a mesh: rep: 16 (over y, x), tp: 16 (over z, core).
Axes of the slice: x: 4, y: 4, z: 8, core: 2. Of those that a mesh axis runs over, the one named last changes fastest.
Arguments:
- inputs: bfloat16 [2, 8192, 8192], P(None, 'rep', 'tp'), may hold values from -6 to 6
- targets: bfloat16 [2, 8192, 2048], P(None, 'rep', 'tp'), may hold values from -6 to 6
- weight: bfloat16 [8192, 2048], P('tp'), may hold values from -0.0625 to 0.0625
- momentum: float32 [16, 8192, 2048], P('rep', 'tp'), may hold values from -0.8 to 0.8
- indices: int32 [2, 16, 64, 16, 2], P(None, None, 'tp'), may hold values from 0 to 127, as said below
Outputs:
- new_weight: bfloat16 [8192, 2048], P('tp')
- new_momentum: float32 [16, 8192, 2048], P('rep', 'tp')
The draws below stay inside these ranges and needn't reach their ends.
Inputs may be any that keep to these rules, and one draw needn't show every extreme that they name: `indices`: the 2 entries of each block's list are distinct rows of the block's transform.
All inputs are finite; a program needn't handle non-finite values.
Results may differ from the reference program's by a relative error of at most 0.0085.
Values may be sent and summed in bfloat16 or wider, within the bound.
A program may use at most 128 MiB of HBM per device.

```python
import jax
import jax.numpy as jnp
from jax import lax

DIN = 8192
DOUT = 2048
BLOCK = 128
STEPS = 2
TOK_DEV = 512
TOKENS = 8192
N_REP = 16


def draw_indices(key, part):
    shape = (STEPS, N_REP, DIN // BLOCK, DOUT // BLOCK)
    first_key, second_key = jax.random.split(jax.random.fold_in(key, 11))
    first = jax.random.randint(first_key, shape, 0, BLOCK)
    offset = jax.random.randint(second_key, shape, 1, BLOCK)
    second = (first + offset) % BLOCK
    anchor = jnp.zeros(shape, jnp.int32).at[0, 0, 0, 0].set(1) == 1
    first = jnp.where(anchor, BLOCK - 1, first)
    second = jnp.where(anchor, 0, second)
    return jnp.stack([first, second], axis=-1).astype(jnp.int32)


def levels(stream_key, dims, pieces, least, high):
    def one(axis_at, shards_of):
        heights = jax.random.uniform(jax.random.fold_in(jax.random.fold_in(stream_key, 6), axis_at), (shards_of,), jnp.float32, least / len(pieces), high / len(pieces))
        return jnp.repeat(jnp.exp(heights), dims[axis_at] // shards_of).reshape((-1,) + (1,) * (len(dims) - axis_at - 1))

    level = one(*pieces[0])
    for cut in pieces[1:]:
        level = level * one(*cut)
    return level


def gaussian(key, shape, deviation, reach, pieces=(), held_as=jnp.bfloat16):
    gain = levels(key, shape, pieces, -0.22, 0.18) if pieces else 1.0
    drawn = jax.random.normal(key, shape, jnp.float32) * deviation * gain
    return jnp.minimum(jnp.maximum(drawn, -reach), reach).astype(held_as)


def setup_inputs(seed: int = 0) -> dict:
    streams_of = jax.random.split(jax.random.key(seed), 6)
    return {
        "inputs": gaussian(streams_of[0], (STEPS, TOKENS, DIN), 1.0, 6.0, ((1, 16), (2, 16))),
        "targets": gaussian(streams_of[1], (STEPS, TOKENS, DOUT), 1.0, 6.0, ((1, 16), (2, 16))),
        "weight": gaussian(streams_of[2], (DIN, DOUT), DIN ** -0.5, 0.0625, ((0, 16),)),
        "momentum": gaussian(streams_of[3], (N_REP, DIN, DOUT), 0.1, 0.8, ((0, 16), (1, 16)), jnp.float32),
        "indices": draw_indices(jax.random.fold_in(streams_of[5], 71), 0),
    }


def dct_table(size):
    rows = jnp.arange(size, dtype=jnp.float32)[:, None]
    cols = jnp.arange(size, dtype=jnp.float32)[None, :]
    scale = jnp.where(rows == 0, jnp.sqrt(1.0 / size), jnp.sqrt(2.0 / size))
    return (scale * jnp.cos(jnp.pi * (2.0 * cols + 1.0) * rows / (2.0 * size))).astype(jnp.float32)

def compress(moment, chosen, basis):
    high = lax.Precision.HIGHEST
    blocks = moment.reshape(DIN // BLOCK, BLOCK, DOUT // BLOCK, BLOCK)
    picks = (chosen[..., None] == jnp.arange(BLOCK, dtype=jnp.int32)).astype(jnp.float32)
    rows_sel = jnp.einsum('abjk,kn->abjn', picks, basis, precision=high)
    inner = jnp.einsum('abjn,anbm->abjm', rows_sel, blocks, precision=high)
    coeffs = jnp.einsum('abjm,cm->abjc', inner, basis, precision=high)
    back = jnp.einsum('abjc,cm->abjm', coeffs, basis, precision=high)
    decoded = jnp.einsum('abjn,abjm->anbm', rows_sel, back, precision=high).reshape(DIN, DOUT)
    return (moment - decoded, decoded)

def reference(inputs, targets, weight, momentum, indices):
    basis = dct_table(BLOCK)
    weight_now = weight
    moments = momentum
    for step in range(STEPS):
        acts = inputs[step].reshape(N_REP, TOK_DEV, DIN)
        goals = targets[step].reshape(N_REP, TOK_DEV, DOUT)

        def replica(total, items):
            acts_r, goals_r, moment, chosen = items
            out = jnp.dot(acts_r, weight_now, preferred_element_type=jnp.float32)
            errors = (out - goals_r.astype(jnp.float32)).astype(jnp.bfloat16)
            grad = lax.dot_general(acts_r, errors, (((0,), (0,)), ((), ())), preferred_element_type=jnp.float32) / TOK_DEV
            kept, decoded = compress(0.9 * moment + grad, chosen, basis)
            return (total + decoded, kept)
        update, moments = lax.scan(replica, jnp.zeros((DIN, DOUT), jnp.float32), (acts, goals, moments, indices[step]))
        weight_now = (weight_now.astype(jnp.float32) - 0.1 * update).astype(jnp.bfloat16)
    return (weight_now, moments)
```

```python
import functools

import jax
import jax.numpy as jnp
import ml_dtypes
import numpy as np
from jax import lax
from jax.experimental import pallas as pl
from jax.experimental.pallas import tpu as pltpu
from jax.sharding import PartitionSpec as P

MESH = pl.DeviceIdType.MESH
BLOCK = 128
STEPS = 2
TOK = 512
NZ = 8
ROWS = 512
NSUB = 4
SUB = TOK // NSUB
F32 = jnp.float32
BF16 = jnp.bfloat16


def basis_parts():
    k = np.arange(BLOCK, dtype=np.float64)[:, None]
    n = np.arange(BLOCK, dtype=np.float64)[None, :]
    scale = np.where(k == 0, np.sqrt(1.0 / BLOCK), np.sqrt(2.0 / BLOCK))
    table = (scale * np.cos(np.pi * (2.0 * n + 1.0) * k / (2.0 * BLOCK))).T
    high = table.astype(ml_dtypes.bfloat16)
    low = (table - high.astype(np.float64)).astype(ml_dtypes.bfloat16)
    return np.stack([high, low])


def iota(shape, axis):
    return lax.broadcasted_iota(jnp.int32, shape, axis)


def kernel(
    n_rep,
    x_ref, t_ref, w_ref, m_ref, idx_ref, bt_ref,
    w_out, m_out,
    xa, xt, tv, wb, mb, ix, ixp, bt, ic, comb, rtf, lu, rtb,
    yp, ys, rl, ef, lx, xr_send, xr_land, rm_send, rm_land, s_send, sn, sall,
    load_sem, pair_send, pair_recv, rs_send, rs_recv, ag_send, ag_recv,
    xr_ssem, xr_rsem, rm_ssem, rm_rsem, sa_ssem, sa_rsem, sp_ssem, sp_rsem,
    pl_ssem, pl_rsem, fw_ssem, fw_rsem, out_sem, outp_ssem, outp_rsem,
):
    r = lax.axis_index("rep")
    me = lax.axis_index("tp")
    z = me // 2
    c = me % 2
    o = 1 - c
    lanes = n_rep * 16
    d = 1 - 2 * c
    partner = {"tp": 2 * z + o}

    def zz(k):
        return lax.rem(z + k + 2 * NZ, NZ)

    long_to = {"tp": 2 * zz(d) + c}
    short_to = {"tp": 2 * zz(-d) + c}

    def remote(src, dst, s, v, dev):
        return pltpu.make_async_remote_copy(
            src_ref=src, dst_ref=dst, send_sem=s, recv_sem=v, device_id=dev, device_id_type=MESH
        )

    def cols(j, h):
        return pl.ds(pl.multiple_of((2 * j + h) * BLOCK, BLOCK), BLOCK)

    half_own = pl.ds(pl.multiple_of(c * ROWS, ROWS), ROWS)
    half_other = pl.ds(pl.multiple_of(o * ROWS, ROWS), ROWS)

    loads = {}

    def load(name, k, src, dst):
        copy = pltpu.make_async_copy(src, dst, load_sem.at[k])
        copy.start()
        loads[name] = copy

    load("x0", 0, x_ref.at[0], xa.at[0, c])
    for j in range(NZ):
        load(("w", j), 8 + j, w_ref.at[:, cols(j, c)], wb.at[j, half_own])
    load("bt", 1, bt_ref, bt)
    load("ix", 2, idx_ref, ix)
    load("x1", 3, x_ref.at[1], xa.at[1, c])
    load("t", 4, t_ref, tv)
    for j in range(NZ):
        load(("m", j), 16 + j, m_ref.at[0, :, pl.ds(2 * BLOCK * j, 2 * BLOCK)], mb.at[j])

    barrier = pltpu.get_barrier_semaphore()
    for k in range(1, 2 * NZ):
        pl.semaphore_signal(barrier, inc=1, device_id={"tp": lax.rem(me + k, 2 * NZ)}, device_id_type=MESH)
    for k in range(1, n_rep):
        pl.semaphore_signal(barrier, inc=1, device_id={"rep": lax.rem(r + k, n_rep)}, device_id_type=MESH)
    pl.semaphore_wait(barrier, 2 * NZ - 1 + n_rep - 1)

    pairs = []

    def pair(k, src, dst):
        copy = remote(src, dst, pair_send.at[k], pair_recv.at[k], partner)
        copy.start()
        pairs.append(copy)

    pair(0, x_ref.at[0], xa.at[0, c])
    for j in range(NZ):
        pair(1 + j, w_ref.at[:, cols(j, o)], wb.at[j, half_own])
    pair(9, idx_ref.at[:, o], ixp)
    pair(10, x_ref.at[1], xa.at[1, c])

    order = [(zz(4 * d), zz(-3 * d)), (zz(3 * d), zz(-2 * d)), (zz(2 * d), zz(-d)), (zz(d), z)]

    def forward(s, k):
        p, q = order[k]
        for i in range(2):
            rows = pl.ds(i * 256, 256)
            acc = jnp.zeros((256, 2 * BLOCK), F32)
            for h in range(2):
                w = jnp.concatenate([wb[p, h * ROWS:(h + 1) * ROWS], wb[q, h * ROWS:(h + 1) * ROWS]], axis=1)
                acc += jnp.dot(xa[s, h, rows], w, preferred_element_type=F32)
            yp[2 * k, rows] = acc[:, :BLOCK]
            yp[2 * k + 1, rows] = acc[:, BLOCK:]
            if k == 0:
                ys[s, 0, rows] = acc[:, :BLOCK].astype(BF16)
                ys[s, 1, rows] = acc[:, BLOCK:].astype(BF16)

    def rs_copy(s, way, h, u):
        slot = h - 1 if way == 0 else 3 + h
        rows = pl.ds(u * SUB, SUB)
        if h == 1:
            src = ys.at[s, way, rows]
        else:
            src = rl.at[s, slot - 1, rows]
        return remote(src, rl.at[s, slot, rows], rs_send.at[s, slot, u], rs_recv.at[s, slot, u], (long_to, short_to)[way])

    def rs_first(s):
        for u in range(NSUB):
            for way in range(2):
                rs_copy(s, way, 1, u).start()

    def rs_hop(s, h):
        for u in range(NSUB):
            rows = pl.ds(u * SUB, SUB)
            for way in range(2):
                if h > 4 - way:
                    continue
                rs_copy(s, way, h - 1, u).wait_recv()
                slot = h - 2 if way == 0 else 2 + h
                rl[s, slot, rows] = (rl[s, slot, rows].astype(F32) + yp[2 * (h - 1) + way, rows]).astype(BF16)
                rs_copy(s, way, h, u).start()

    def rs_last(s):
        for u in range(NSUB):
            rows = pl.ds(u * SUB, SUB)
            rs_copy(s, 1, 3, u).wait_recv()
            rs_copy(s, 0, 4, u).wait_recv()
            total = yp[7, rows] + rl[s, 3, rows].astype(F32) + rl[s, 6, rows].astype(F32)
            ef[s, c, z, rows] = (total - tv[s, rows].astype(F32)).astype(BF16)

    def ag_copy(s, way, h, u):
        slot = h - 1 if way == 0 else 3 + h
        rows = pl.ds(u * SUB, SUB)
        origin = zz(-d * (h - 1)) if way == 0 else zz(d * (h - 1))
        block = ef.at[s, c, origin, rows]
        return remote(block, block, ag_send.at[s, slot, u], ag_recv.at[s, slot, u], (long_to, short_to)[way])

    def fw_copy(s, k):
        origin = zz(-d * k) if k < 5 else zz(d * (k - 4))
        block = ef.at[s, c, origin]
        return remote(block, block, fw_ssem.at[s, k], fw_rsem.at[s, k], partner)

    def ag_hop(s, h):
        for u in range(NSUB):
            for way in range(2):
                if h > 1 and h <= 5 - way:
                    ag_copy(s, way, h - 1, u).wait_recv()
                if h <= 4 - way:
                    ag_copy(s, way, h, u).start()
        if h == 1:
            fw_copy(s, 0).start()
        else:
            for way in range(2):
                if h <= 5 - way:
                    fw_copy(s, h - 1 if way == 0 else 3 + h).start()

    def build_replicas(s):
        def body(j, _):
            row = ix[s, c, pl.ds(j, 1)] + ixp[s, pl.ds(j, 1)]
            onehot = jnp.where(iota((BLOCK, lanes), 0) == row, 1.0, 0.0).astype(BF16)
            kept = jnp.dot(bt[0], onehot, preferred_element_type=F32)
            rtb[s, j] = kept.astype(BF16)
            for a in range(8):
                mine = (iota((BLOCK, lanes), 1) % 16) // 2 == a
                lu[s, j, a * BLOCK:(a + 1) * BLOCK] = jnp.where(mine, kept, 0.0).astype(BF16)
            return 0

        lax.fori_loop(0, NZ, body, 0)

    def build_rows(s):
        def body(j, _):
            pick = jnp.where(iota((16, lanes), 1) == 16 * r + iota((16, lanes), 0), 1.0, 0.0).astype(BF16)
            kept = lax.dot_general(pick, rtb[s, j], (((1,), (1,)), ((), ())), preferred_element_type=F32)
            for a in range(8):
                lx[j, :, a * BLOCK:(a + 1) * BLOCK] = jnp.where(iota((16, BLOCK), 0) // 2 == a, kept, 0.0).astype(BF16)
            return 0

        lax.fori_loop(0, NZ, body, 0)
        table = lx[...].reshape(NZ * 16, 2 * ROWS)
        out = jnp.zeros((NZ * 16, TOK), F32)
        for h in range(2):
            out += lax.dot_general(
                table[:, h * ROWS:(h + 1) * ROWS], xa[s, h], (((1,), (1,)), ((), ())), preferred_element_type=F32
            )
        xr_send[s] = out.astype(BF16).reshape(NZ, 16, TOK)

    def xr_copy(s, k):
        to = zz(k)
        return remote(
            xr_send.at[s, to], xr_land.at[s, z], xr_ssem.at[s, k], xr_rsem.at[s, k], {"tp": 2 * to + c}
        )

    def build_own(s):
        lane = iota((NZ, BLOCK), 1)
        shift = lax.rem(2 * lanes - 16 * r - 8 * c, lanes)
        first = pltpu.roll(ix[s, 0], shift, 1)[:, :BLOCK]
        second = pltpu.roll(ix[s, 1], shift, 1)[:, :BLOCK]
        ic[s] = jnp.where(
            lane < 8,
            first,
            jnp.where(
                lane < 16,
                pltpu.roll(first, 8, 1),
                jnp.where(lane < 24, pltpu.roll(second, 16, 1), jnp.where(lane < 32, pltpu.roll(second, 24, 1), -1)),
            ),
        )

        def body(j, _):
            row = ic[s, pl.ds(j, 1)]
            lane = iota((BLOCK, BLOCK), 1)
            hit = iota((BLOCK, BLOCK), 0) == row
            even = (lane // 8) % 2 == 0
            high = jnp.where(hit & even, 1.0, 0.0).astype(BF16)
            low = jnp.where(hit & jnp.logical_not(even), 1.0, 0.0).astype(BF16)
            both = jnp.dot(bt[0], high, preferred_element_type=F32) + jnp.dot(bt[1], low, preferred_element_type=F32)
            comb[s, j] = both
            rtf[s, j] = both + pltpu.roll(both, BLOCK - 8, 1)
            return 0

        lax.fori_loop(0, NZ, body, 0)

    def project(s):
        def body(j, _):
            for h in range(2):
                for a in range(4):
                    block = mb[j, a * BLOCK:(a + 1) * BLOCK, h * BLOCK:(h + 1) * BLOCK]
                    for k in range(2):
                        lane = 16 * h + 2 * a + k
                        column = rtf[s, j, :, lane:lane + 1]
                        rm_send[s, j, h, 2 * a + k:2 * a + k + 1] = jnp.sum(block * column, axis=0, keepdims=True)
            return 0

        lax.fori_loop(0, NZ, body, 0)

    def rm_copy(s, k):
        to = lax.rem(me + k, 2 * NZ)
        return remote(
            rm_send.at[s, to // 2, to % 2], rm_land.at[s, me], rm_ssem.at[s, k], rm_rsem.at[s, k], {"tp": to}
        )

    def kept_rows(s):
        for k in range(1, NZ):
            xr_copy(s, k).wait_recv()
        for k in range(1, 2 * NZ):
            rm_copy(s, k).wait_recv()
        xr_land[s, z] = xr_send[s, z]
        rm_land[s, me] = rm_send[s, z, c]
        table = xr_land[s].reshape(NZ * 16, TOK)
        out = jnp.dot(table, ef[s, c, z], preferred_element_type=F32) * (1.0 / TOK)
        out += 0.9 * rm_land[s].reshape(NZ * 16, BLOCK)
        s_send[s] = out.astype(BF16).reshape(NZ, 16, BLOCK)

    def sa_copy(s, k):
        to = zz(k)
        return remote(
            s_send.at[s, to], sn.at[s, c, z], sa_ssem.at[s, k], sa_rsem.at[s, k], {"tp": 2 * to + c}
        )

    def sp_copy(s):
        return remote(sn.at[s, c], sn.at[s, c], sp_ssem.at[s], sp_rsem.at[s], partner)

    def pl_copy(s, k):
        return remote(
            sn.at[s, c], sall.at[s, r], pl_ssem.at[s, k], pl_rsem.at[s, k], {"rep": lax.rem(r + k, n_rep)}
        )

    def share(s):
        for k in range(1, NZ):
            sa_copy(s, k).start()
        sn[s, c, z] = s_send[s, z]

    def spread(s):
        for k in range(1, NZ):
            sa_copy(s, k).wait_recv()
        for k in range(1, n_rep):
            pl_copy(s, k).start()
        sp_copy(s).start()
        sall[s, r] = sn[s, c]

    def collect(s):
        for k in range(1, n_rep):
            pl_copy(s, k).wait_recv()

    def update(s, j):
        stack = sall[s, :, j].reshape(lanes, BLOCK)
        for i in range(4):
            rows = pl.ds(i * 256, 256)
            change = jnp.dot(lu[s, j, rows], stack, preferred_element_type=F32)
            wb[j, rows] = (wb[j, rows].astype(F32) - 0.1 * change).astype(BF16)

    def momentum(s, j):
        e = jnp.concatenate([ef[s, 0, j], ef[s, 1, j]], axis=1)
        parts = []
        for h in range(2):
            both = sn[s, h, j].astype(F32)
            parts.append(jnp.where(c == 0, both[:8], both[8:]))
        zero = jnp.zeros((8, BLOCK), F32)
        top = jnp.concatenate([parts[0], zero], axis=1)
        low = jnp.concatenate([zero, parts[1]], axis=1)
        right = jnp.concatenate([top, top, low, low, jnp.zeros((BLOCK - 32, 2 * BLOCK), F32)], axis=0).astype(BF16)
        lane = iota((BLOCK, BLOCK), 1)
        for a in range(4):
            rows = pl.ds(a * BLOCK, BLOCK)
            grad = jnp.dot(xt[s, rows], e, preferred_element_type=F32)
            left = jnp.where((lane % 8) // 2 == a, comb[s, j], 0.0).astype(BF16)
            taken = jnp.dot(left, right, preferred_element_type=F32)
            mb[j, rows] = 0.9 * mb[j, rows] + grad * (1.0 / TOK) - taken

    def fw_wait(s):
        for k in range(NZ):
            fw_copy(s, k).wait_recv()

    def turn(s):
        xt[s] = xa[s, c].T

    loads["x0"].wait()
    pairs[0].wait_recv()
    for j in range(NZ):
        loads["w", j].wait()
        pairs[1 + j].wait_recv()
    forward(0, 0)
    rs_first(0)
    loads["bt"].wait()
    loads["ix"].wait()
    pairs[9].wait_recv()
    build_replicas(0)
    build_rows(0)
    for k in range(1, NZ):
        xr_copy(0, k).start()
    for k in range(1, 4):
        forward(0, k)
    rs_hop(0, 2)
    build_own(0)
    for j in range(NZ):
        loads["m", j].wait()
    project(0)
    for k in range(1, 2 * NZ):
        rm_copy(0, k).start()
    rs_hop(0, 3)
    loads["x1"].wait()
    pairs[10].wait_recv()
    build_replicas(1)
    build_rows(1)
    rs_hop(0, 4)
    build_own(1)
    turn(0)
    loads["t"].wait()
    rs_last(0)
    kept_rows(0)
    share(0)
    ag_hop(0, 1)
    spread(0)
    ag_hop(0, 2)
    for k in range(1, NZ):
        xr_copy(1, k).start()
    turn(1)
    collect(0)

    for k in range(4):
        update(0, order[k][0])
        update(0, order[k][1])
        forward(1, k)
        if k == 0:
            rs_first(1)
            ag_hop(0, 3)
    ag_hop(0, 4)
    rs_hop(1, 2)
    ag_hop(0, 5)
    fw_wait(0)
    sp_copy(0).wait_recv()
    lax.fori_loop(0, NZ, lambda j, _: (momentum(0, j), 0)[1], 0)
    rs_hop(1, 3)
    project(1)
    for k in range(1, 2 * NZ):
        rm_copy(1, k).start()
    rs_hop(1, 4)
    rs_last(1)
    kept_rows(1)
    share(1)
    ag_hop(1, 1)
    spread(1)
    ag_hop(1, 2)
    ag_hop(1, 3)
    collect(1)
    out_copies = []
    for j in range(NZ):
        update(1, j)
        own = pltpu.make_async_copy(wb.at[j, half_own], w_out.at[:, cols(j, c)], out_sem.at[j])
        own.start()
        other = remote(wb.at[j, half_other], w_out.at[:, cols(j, c)], outp_ssem.at[j], outp_rsem.at[j], partner)
        other.start()
        out_copies += [own, other]
    ag_hop(1, 4)
    ag_hop(1, 5)
    fw_wait(1)
    sp_copy(1).wait_recv()

    def finish(j, _):
        momentum(1, j)
        pltpu.make_async_copy(
            mb.at[j], m_out.at[0, :, pl.ds(pl.multiple_of(2 * BLOCK * j, 2 * BLOCK), 2 * BLOCK)], out_sem.at[NZ + j]
        ).start()
        return 0

    lax.fori_loop(0, NZ, finish, 0)

    for copy in out_copies:
        copy.wait()
    for j in range(NZ):
        pltpu.make_async_copy(mb.at[j], m_out.at[0, :, pl.ds(2 * BLOCK * j, 2 * BLOCK)], out_sem.at[NZ + j]).wait()
    for copy in pairs:
        copy.wait_send()
    for s in range(STEPS):
        for way in range(2):
            for h in range(1, 5 - way):
                for u in range(NSUB):
                    rs_copy(s, way, h, u).wait_send()
                    ag_copy(s, way, h, u).wait_send()
        for k in range(NZ):
            fw_copy(s, k).wait_send()
        for k in range(1, NZ):
            xr_copy(s, k).wait_send()
            sa_copy(s, k).wait_send()
        for k in range(1, 2 * NZ):
            rm_copy(s, k).wait_send()
        for k in range(1, n_rep):
            pl_copy(s, k).wait_send()
        sp_copy(s).wait_send()


def local(n_rep, inputs, targets, weight, momentum, indices):
    core = lax.axis_index("tp") % 2
    lanes = n_rep * 16
    own = indices.reshape(STEPS, n_rep, 4, NZ, 2, 2).transpose(0, 4, 3, 1, 2, 5)[:, :, :, :, None]
    place = jnp.arange(2, dtype=jnp.int32)[:, None, None] == core
    arranged = jnp.where(place, own, 0).reshape(STEPS, 2, NZ, lanes)
    any_space = pl.BlockSpec(memory_space=pl.ANY)
    dma = pltpu.SemaphoreType.DMA
    scratch = [
        pltpu.VMEM((STEPS, 2, TOK, ROWS), BF16),
        pltpu.VMEM((STEPS, ROWS, TOK), BF16),
        pltpu.VMEM((STEPS, TOK, BLOCK), BF16),
        pltpu.VMEM((NZ, 2 * ROWS, BLOCK), BF16),
        pltpu.VMEM((NZ, ROWS, 2 * BLOCK), F32),
        pltpu.VMEM((STEPS, 2, NZ, lanes), jnp.int32),
        pltpu.VMEM((STEPS, NZ, lanes), jnp.int32),
        pltpu.VMEM((2, BLOCK, BLOCK), BF16),
        pltpu.VMEM((STEPS, NZ, BLOCK), jnp.int32),
        pltpu.VMEM((STEPS, NZ, BLOCK, BLOCK), F32),
        pltpu.VMEM((STEPS, NZ, BLOCK, BLOCK), F32),
        pltpu.VMEM((STEPS, NZ, 2 * ROWS, lanes), BF16),
        pltpu.VMEM((STEPS, NZ, BLOCK, lanes), BF16),
        pltpu.VMEM((NZ, TOK, BLOCK), F32),
        pltpu.VMEM((STEPS, 2, TOK, BLOCK), BF16),
        pltpu.VMEM((STEPS, 7, TOK, BLOCK), BF16),
        pltpu.VMEM((STEPS, 2, NZ, TOK, BLOCK), BF16),
        pltpu.VMEM((NZ, 16, 2 * ROWS), BF16),
        pltpu.VMEM((STEPS, NZ, 16, TOK), BF16),
        pltpu.VMEM((STEPS, NZ, 16, TOK), BF16),
        pltpu.VMEM((STEPS, NZ, 2, 8, BLOCK), F32),
        pltpu.VMEM((STEPS, 2 * NZ, 8, BLOCK), F32),
        pltpu.VMEM((STEPS, NZ, 16, BLOCK), BF16),
        pltpu.VMEM((STEPS, 2, NZ, 16, BLOCK), BF16),
        pltpu.VMEM((STEPS, n_rep, NZ, 16, BLOCK), BF16),
        dma((24,)), dma((11,)), dma((11,)),
        dma((STEPS, 7, NSUB)), dma((STEPS, 7, NSUB)), dma((STEPS, 7, NSUB)), dma((STEPS, 7, NSUB)),
        dma((STEPS, NZ)), dma((STEPS, NZ)), dma((STEPS, 2 * NZ)), dma((STEPS, 2 * NZ)),
        dma((STEPS, NZ)), dma((STEPS, NZ)), dma((STEPS,)), dma((STEPS,)),
        dma((STEPS, n_rep)), dma((STEPS, n_rep)), dma((STEPS, NZ)), dma((STEPS, NZ)),
        dma((2 * NZ,)), dma((NZ,)), dma((NZ,)),
    ]
    return pl.pallas_call(
        functools.partial(kernel, n_rep),
        out_shape=(
            jax.ShapeDtypeStruct(weight.shape, BF16),
            jax.ShapeDtypeStruct(momentum.shape, F32),
        ),
        in_specs=[any_space] * 6,
        out_specs=(any_space, any_space),
        scratch_shapes=scratch,
        compiler_params=pltpu.CompilerParams(
            collective_id=0, has_side_effects=True, vmem_limit_bytes=56 << 20
        ),
    )(inputs, targets, weight, momentum, arranged, jnp.asarray(basis_parts()))


def solution(mesh):
    in_specs = (
        P(None, "rep", "tp"),
        P(None, "rep", "tp"),
        P("tp", None),
        P("rep", "tp", None),
        P(None, None, "tp", None, None),
    )
    out_specs = (P("tp", None), P("rep", "tp", None))
    return jax.shard_map(
        functools.partial(local, mesh.shape["rep"]), mesh=mesh, in_specs=in_specs, out_specs=out_specs, check_vma=False
    )
```

```python
import functools

import jax
import jax.numpy as jnp
import ml_dtypes
import numpy as np
from jax import lax
from jax.experimental import pallas as pl
from jax.experimental.pallas import tpu as pltpu
from jax.sharding import PartitionSpec as P

MESH = pl.DeviceIdType.MESH
BLOCK = 128
STEPS = 2
TOK = 512
NZ = 8
ROWS = 512
NSUB = 4
SUB = TOK // NSUB
F32 = jnp.float32
BF16 = jnp.bfloat16


def basis_parts():
    k = np.arange(BLOCK, dtype=np.float64)[:, None]
    n = np.arange(BLOCK, dtype=np.float64)[None, :]
    scale = np.where(k == 0, np.sqrt(1.0 / BLOCK), np.sqrt(2.0 / BLOCK))
    table = (scale * np.cos(np.pi * (2.0 * n + 1.0) * k / (2.0 * BLOCK))).T
    high = table.astype(ml_dtypes.bfloat16)
    low = (table - high.astype(np.float64)).astype(ml_dtypes.bfloat16)
    return np.stack([high, low])


def iota(shape, axis):
    return lax.broadcasted_iota(jnp.int32, shape, axis)


def kernel(
    n_rep,
    x_ref, t_ref, w_ref, m_ref, idx_ref, bt_ref,
    w_out, m_out,
    xa, xt, tv, wb, mb, iv, bt, frow, left, prow, lu,
    yp, ys, rl, ef, lx, xr_send, xr_land, rm_send, rm_land, s_send, sn, sall,
    load_sem, pair_send, pair_recv, rs_send, rs_recv, ag_send, ag_recv,
    xr_ssem, xr_rsem, rm_ssem, rm_rsem, sa_ssem, sa_rsem, sp_ssem, sp_rsem,
    pl_ssem, pl_rsem, fw_ssem, fw_rsem, out_sem, outp_ssem, outp_rsem,
):
    r = lax.axis_index("rep")
    me = lax.axis_index("tp")
    z = me // 2
    c = me % 2
    o = 1 - c
    lanes = n_rep * 16
    d = 1 - 2 * c
    partner = {"tp": 2 * z + o}

    def zz(k):
        return lax.rem(z + k + 2 * NZ, NZ)

    long_to = {"tp": 2 * zz(d) + c}
    short_to = {"tp": 2 * zz(-d) + c}

    def remote(src, dst, s, v, dev):
        return pltpu.make_async_remote_copy(
            src_ref=src, dst_ref=dst, send_sem=s, recv_sem=v, device_id=dev, device_id_type=MESH
        )

    def cols(j, h):
        return pl.ds(pl.multiple_of((2 * j + h) * BLOCK, BLOCK), BLOCK)

    half_own = pl.ds(pl.multiple_of(c * ROWS, ROWS), ROWS)
    half_other = pl.ds(pl.multiple_of(o * ROWS, ROWS), ROWS)

    loads = {}

    def load(name, k, src, dst):
        copy = pltpu.make_async_copy(src, dst, load_sem.at[k])
        copy.start()
        loads[name] = copy

    steps_out = (4, -3, 3, -2, 2, -1, 1, 0)
    load("x0", 0, x_ref.at[0], xa.at[0, c])
    for i in range(NZ):
        j = zz(d * steps_out[i])
        load(("w", i), 8 + i, w_ref.at[:, cols(j, c)], wb.at[j, half_own])
    load("ix", 2, idx_ref, iv.at[c])
    load("bt", 1, bt_ref, bt)
    load("x1", 3, x_ref.at[1], xa.at[1, c])
    load("t", 4, t_ref, tv)
    for j in range(NZ):
        load(("m", j), 16 + j, m_ref.at[0, :, pl.ds(2 * BLOCK * j, 2 * BLOCK)], mb.at[j])

    barrier = pltpu.get_barrier_semaphore()
    for k in range(1, 2 * NZ):
        pl.semaphore_signal(barrier, inc=1, device_id={"tp": lax.rem(me + k, 2 * NZ)}, device_id_type=MESH)
    for k in range(1, n_rep):
        pl.semaphore_signal(barrier, inc=1, device_id={"rep": lax.rem(r + k, n_rep)}, device_id_type=MESH)
    pl.semaphore_wait(barrier, 2 * NZ - 1 + n_rep - 1)

    pairs = []

    def pair(k, src, dst):
        copy = remote(src, dst, pair_send.at[k], pair_recv.at[k], partner)
        copy.start()
        pairs.append(copy)

    pair(0, x_ref.at[0], xa.at[0, c])
    for i in range(NZ):
        j = zz(-d * steps_out[i])
        pair(1 + i, w_ref.at[:, cols(j, o)], wb.at[j, half_own])
    pair(9, idx_ref, iv.at[c])
    pair(10, x_ref.at[1], xa.at[1, c])

    order = [(zz(4 * d), zz(-3 * d)), (zz(3 * d), zz(-2 * d)), (zz(2 * d), zz(-d)), (zz(d), z)]

    def forward(s, k):
        p, q = order[k]
        for i in range(2):
            rows = pl.ds(i * 256, 256)
            acc = jnp.zeros((256, 2 * BLOCK), F32)
            for h in range(2):
                w = jnp.concatenate([wb[p, h * ROWS:(h + 1) * ROWS], wb[q, h * ROWS:(h + 1) * ROWS]], axis=1)
                acc += jnp.dot(xa[s, h, rows], w, preferred_element_type=F32)
            yp[2 * k, rows] = acc[:, :BLOCK]
            yp[2 * k + 1, rows] = acc[:, BLOCK:]
            if k == 0:
                ys[s, 0, rows] = acc[:, :BLOCK].astype(BF16)
                ys[s, 1, rows] = acc[:, BLOCK:].astype(BF16)

    def rs_copy(s, way, h, u):
        slot = h - 1 if way == 0 else 3 + h
        rows = pl.ds(u * SUB, SUB)
        if h == 1:
            src = ys.at[s, way, rows]
        else:
            src = rl.at[s, slot - 1, rows]
        return remote(src, rl.at[s, slot, rows], rs_send.at[s, slot, u], rs_recv.at[s, slot, u], (long_to, short_to)[way])

    def rs_first(s):
        for u in range(NSUB):
            for way in range(2):
                rs_copy(s, way, 1, u).start()

    def rs_wave(s, h, u):
        rows = pl.ds(u * SUB, SUB)
        for way in range(2):
            if h > 4 - way:
                continue
            rs_copy(s, way, h - 1, u).wait_recv()
            slot = h - 2 if way == 0 else 2 + h
            rl[s, slot, rows] = (rl[s, slot, rows].astype(F32) + yp[2 * (h - 1) + way, rows]).astype(BF16)
            rs_copy(s, way, h, u).start()

    def rs_last(s, u):
        rows = pl.ds(u * SUB, SUB)
        rs_copy(s, 1, 3, u).wait_recv()
        rs_copy(s, 0, 4, u).wait_recv()
        total = yp[7, rows] + rl[s, 3, rows].astype(F32) + rl[s, 6, rows].astype(F32)
        ef[s, c, z, rows] = (total - tv[s, rows].astype(F32)).astype(BF16)

    def rs_rest(s, work):
        for h in range(2, 5):
            for u in range(NSUB):
                rs_wave(s, h, u)
                run(work, 1)
        for u in range(NSUB):
            rs_last(s, u)
        run(work, len(work))

    def ag_copy(s, way, h, u):
        slot = h - 1 if way == 0 else 3 + h
        rows = pl.ds(u * SUB, SUB)
        origin = zz(-d * (h - 1)) if way == 0 else zz(d * (h - 1))
        block = ef.at[s, c, origin, rows]
        return remote(block, block, ag_send.at[s, slot, u], ag_recv.at[s, slot, u], (long_to, short_to)[way])

    def fw_copy(s, q):
        block = ef.at[s, c, zz(d * q)]
        k = q + 4 if q > -4 else 8
        return remote(block, block, fw_ssem.at[s, k], fw_rsem.at[s, k], partner)

    def fw_arrival(s, q):
        block = ef.at[s, o, zz(d * q)]
        k = 4 - q if q < 4 else 8
        return remote(block, block, fw_ssem.at[s, k], fw_rsem.at[s, k], partner)

    def ag_wave(s, h, u):
        for way in range(2):
            if h > 1 and h <= 5 - way:
                ag_copy(s, way, h - 1, u).wait_recv()
            if h <= 4 - way:
                ag_copy(s, way, h, u).start()
        if u == NSUB - 1:
            if h == 1:
                fw_copy(s, 0).start()
            else:
                fw_copy(s, 1 - h).start()
                if h <= 4:
                    fw_copy(s, h - 1).start()

    def ag_hop(s, h, work=()):
        for u in range(NSUB):
            ag_wave(s, h, u)
            run(work, 1)

    def arrange(s):
        pick = jnp.where(iota((NZ, 16), 1) == 2 * iota((NZ, 16), 0) + c, 1.0, 0.0).astype(BF16)
        half = n_rep * 8
        source = iota((half, lanes), 0)
        place = iota((half, lanes), 1)
        total = jnp.zeros((NZ, lanes), F32)
        for h in range(2):
            turned = lax.dot_general(
                pick, iv[h, s].astype(F32).astype(BF16), (((1,), (1,)), ((), ())), preferred_element_type=F32
            )
            to = jnp.where(place == (source // 8) * 16 + h * 8 + source % 8, 1.0, 0.0).astype(BF16)
            total += jnp.dot(turned.astype(BF16), to, preferred_element_type=F32)
        frow[s] = total

    def build_replicas(s, j):
        onehot = jnp.where(iota((BLOCK, lanes), 0).astype(F32) == frow[s, pl.ds(j, 1)], 1.0, 0.0).astype(BF16)
        kept = jnp.dot(bt[0], onehot, preferred_element_type=F32)
        for a in range(8):
            mine = (iota((BLOCK, lanes), 1) % 16) // 2 == a
            lu[s, j, a * BLOCK:(a + 1) * BLOCK] = jnp.where(mine, kept, 0.0).astype(BF16)

    def build_rows(s):
        lane = iota((lanes, BLOCK), 1)
        own = jnp.where(iota((lanes, BLOCK), 0) == 16 * r + lane % 16, 1.0, 0.0).astype(BF16)
        spread_rows = jnp.dot(frow[s].astype(BF16), own, preferred_element_type=F32)
        flat = jnp.where(iota((NZ, BLOCK), 1) // 16 == iota((NZ, BLOCK), 0), spread_rows, 0.0)
        row = jnp.sum(flat, axis=0, keepdims=True)
        onehot = jnp.where(iota((BLOCK, BLOCK), 0).astype(F32) == row, 1.0, 0.0).astype(BF16)
        kept = jnp.dot(bt[0], onehot, preferred_element_type=F32).T
        out = jnp.zeros((NZ * 16, TOK), F32)
        for h in range(2):
            for a in range(4):
                mine = (iota((BLOCK, BLOCK), 0) % 16) // 2 == 4 * h + a
                lx[:, a * BLOCK:(a + 1) * BLOCK] = jnp.where(mine, kept, 0.0).astype(BF16)
            out += lax.dot_general(lx[...], xa[s, h], (((1,), (1,)), ((), ())), preferred_element_type=F32)
        xr_send[s] = out.astype(BF16).reshape(NZ, 16, TOK)

    def xr_copy(s, k):
        to = zz(k)
        return remote(
            xr_send.at[s, to], xr_land.at[s, z], xr_ssem.at[s, k], xr_rsem.at[s, k], {"tp": 2 * to + c}
        )

    def build_own(s, g):
        mine = iv[c, s, pl.ds(pl.multiple_of(8 * r, 8), 8)].astype(F32).astype(BF16)
        lane = iota((16, BLOCK), 1)
        to = jnp.where(iota((16, BLOCK), 0) == 8 * g + lane // 16, 1.0, 0.0).astype(BF16)
        wide = jnp.dot(mine, to, preferred_element_type=F32)
        flat = jnp.where(iota((8, BLOCK), 1) % 8 == iota((8, BLOCK), 0), wide, 0.0)
        row = jnp.sum(flat, axis=0, keepdims=True)
        lane = iota((BLOCK, BLOCK), 1)
        hit = iota((BLOCK, BLOCK), 0).astype(F32) == row
        even = (lane // 8) % 2 == 0
        high = jnp.where(hit & even, 1.0, 0.0).astype(BF16)
        low = jnp.where(hit & jnp.logical_not(even), 1.0, 0.0).astype(BF16)
        both = jnp.dot(bt[0], high, preferred_element_type=F32) + jnp.dot(bt[1], low, preferred_element_type=F32)
        turned = both.T
        for a in range(4):
            left[s, g, a * BLOCK:(a + 1) * BLOCK] = jnp.where((lane % 8) // 2 == a, both, 0.0).astype(BF16)
            rows = jnp.where((iota((BLOCK, BLOCK), 0) % 8) // 2 == a, turned, 0.0).astype(BF16)
            prow[s, 4 * g:4 * g + 4, :, a * BLOCK:(a + 1) * BLOCK] = rows.reshape(4, 32, BLOCK)

    def project(s, j):
        table = prow[s, j]
        values = mb[j]
        high = values.astype(BF16)
        low = (values - high.astype(F32)).astype(BF16)
        out = jnp.dot(table, high, preferred_element_type=F32) + jnp.dot(table, low, preferred_element_type=F32)
        rm_send[s, j, 0] = out[0:8, :BLOCK] + out[8:16, :BLOCK]
        rm_send[s, j, 1] = out[16:24, BLOCK:] + out[24:32, BLOCK:]

    def rm_copy(s, k):
        to = lax.rem(me + k, 2 * NZ)
        return remote(
            rm_send.at[s, to // 2, to % 2], rm_land.at[s, me], rm_ssem.at[s, k], rm_rsem.at[s, k], {"tp": to}
        )

    def kept_rows(s):
        for k in range(1, NZ):
            xr_copy(s, k).wait_recv()
        for k in range(1, 2 * NZ):
            rm_copy(s, k).wait_recv()
        xr_land[s, z] = xr_send[s, z]
        rm_land[s, me] = rm_send[s, z, c]
        table = xr_land[s].reshape(NZ * 16, TOK)
        out = jnp.dot(table, ef[s, c, z], preferred_element_type=F32) * (1.0 / TOK)
        out += 0.9 * rm_land[s].reshape(NZ * 16, BLOCK)
        s_send[s] = out.astype(BF16).reshape(NZ, 16, BLOCK)

    def sa_copy(s, k):
        to = zz(k)
        return remote(
            s_send.at[s, to], sn.at[s, c, z], sa_ssem.at[s, k], sa_rsem.at[s, k], {"tp": 2 * to + c}
        )

    def sp_copy(s):
        return remote(sn.at[s, c], sn.at[s, c], sp_ssem.at[s], sp_rsem.at[s], partner)

    def pl_copy(s, k):
        return remote(
            sn.at[s, c], sall.at[s, r], pl_ssem.at[s, k], pl_rsem.at[s, k], {"rep": lax.rem(r + k, n_rep)}
        )

    def share(s):
        for k in range(1, NZ):
            sa_copy(s, k).start()
        sn[s, c, z] = s_send[s, z]

    def spread(s):
        for k in range(1, NZ):
            sa_copy(s, k).wait_recv()
        for k in range(1, n_rep):
            pl_copy(s, k).start()
        sp_copy(s).start()
        sall[s, r] = sn[s, c]

    def collect(s):
        for k in range(1, n_rep):
            pl_copy(s, k).wait_recv()

    def update(s, j):
        stack = sall[s, :, j].reshape(lanes, BLOCK)
        for i in range(4):
            rows = pl.ds(i * 256, 256)
            change = jnp.dot(lu[s, j, rows], stack, preferred_element_type=F32)
            wb[j, rows] = (wb[j, rows].astype(F32) - 0.1 * change).astype(BF16)

    def momentum(s, q):
        fw_arrival(s, q).wait_recv()
        j = zz(d * q)
        e = jnp.concatenate([ef[s, 0, j], ef[s, 1, j]], axis=1)
        parts = []
        for h in range(2):
            both = sn[s, h, j].astype(F32)
            parts.append(jnp.where(c == 0, both[:8], both[8:]))
        zero = jnp.zeros((8, BLOCK), F32)
        top = jnp.concatenate([parts[0], zero], axis=1)
        low = jnp.concatenate([zero, parts[1]], axis=1)
        block = jnp.concatenate([top, top, low, low], axis=0)
        right = jnp.concatenate([jnp.where(j % 4 == i, block, 0.0) for i in range(4)], axis=0).astype(BF16)
        for i in range(2):
            rows = pl.ds(i * 256, 256)
            grad = jnp.dot(xt[s, rows], e, preferred_element_type=F32)
            taken = jnp.dot(left[s, j // 4, rows], right, preferred_element_type=F32)
            mb[j, rows] = 0.9 * mb[j, rows] + grad * (1.0 / TOK) - taken

    def gain(q):
        momentum(0, q)
        project(1, zz(d * q))

    def finish(q):
        momentum(1, q)
        j = zz(d * q)
        m_copy(j).start()

    def m_copy(j):
        columns = pl.ds(pl.multiple_of(2 * BLOCK * j, 2 * BLOCK), 2 * BLOCK)
        return pltpu.make_async_copy(mb.at[j], m_out.at[0, :, columns], out_sem.at[NZ + j])

    def run(work, count):
        for _ in range(min(count, len(work))):
            work.pop(0)()

    def turn(s):
        xt[s] = xa[s, c].T

    loads["x0"].wait()
    pairs[0].wait_recv()

    def ready(k):
        for i in (2 * k, 2 * k + 1):
            loads["w", i].wait()
            pairs[1 + i].wait_recv()

    ready(0)
    forward(0, 0)
    rs_first(0)
    ready(1)
    forward(0, 1)
    loads["bt"].wait()
    loads["ix"].wait()
    pairs[9].wait_recv()
    arrange(0)
    build_rows(0)
    for k in range(1, NZ):
        xr_copy(0, k).start()
    ready(2)
    ready(3)

    def first_products():
        for j in range(NZ):
            loads["m", j].wait()
        project(0, 0)

    def send_products(s):
        for k in range(1, 2 * NZ):
            rm_copy(s, k).start()

    def last_products():
        project(0, 7)
        send_products(0)

    def second_rows():
        loads["x1"].wait()
        pairs[10].wait_recv()
        arrange(1)
        build_rows(1)

    def two(f, s, j):
        return lambda: (f(s, j), f(s, j + 1))

    rs_rest(0, [
        lambda: forward(0, 2),
        lambda: build_own(0, 0),
        lambda: (build_own(0, 1), loads["t"].wait()),
        lambda: forward(0, 3),
        first_products,
        lambda: (project(0, 1), project(0, 2)),
        lambda: (project(0, 3), project(0, 4)),
        lambda: (project(0, 5), project(0, 6)),
        last_products,
        two(build_replicas, 0, 0),
        two(build_replicas, 0, 2),
        two(build_replicas, 0, 4),
    ])
    kept_rows(0)
    share(0)
    ag_hop(0, 1)
    two(build_replicas, 0, 6)()
    turn(0)
    second_rows()
    spread(0)
    ag_hop(0, 2)
    for k in range(1, NZ):
        xr_copy(1, k).start()
    build_own(1, 0)
    build_own(1, 1)
    sp_copy(0).wait_recv()
    gain(0)
    ag_hop(0, 3)
    collect(0)

    for k in range(4):
        update(0, order[k][0])
        update(0, order[k][1])
        forward(1, k)
        if k == 0:
            rs_first(1)
        if k == 1:
            ag_hop(0, 4)

    def last_gain():
        gain(4)
        send_products(1)

    rs_rest(1, [
        lambda: gain(1),
        lambda: gain(-1),
        lambda: gain(2),
        lambda: gain(-2),
        lambda: (ag_hop(0, 5), gain(3)),
        lambda: gain(-3),
        last_gain,
        lambda: turn(1),
        two(build_replicas, 1, 0),
        two(build_replicas, 1, 2),
        two(build_replicas, 1, 4),
        two(build_replicas, 1, 6),
    ])
    kept_rows(1)
    share(1)
    ag_hop(1, 1)
    spread(1)
    ag_hop(1, 2)
    sp_copy(1).wait_recv()
    ag_hop(1, 3, [lambda: finish(0), lambda: finish(1), lambda: finish(-1)])
    collect(1)
    out_copies = []

    def new_weight(j):
        update(1, j)
        own = pltpu.make_async_copy(wb.at[j, half_own], w_out.at[:, cols(j, c)], out_sem.at[j])
        own.start()
        other = remote(wb.at[j, half_other], w_out.at[:, cols(j, c)], outp_ssem.at[j], outp_rsem.at[j], partner)
        other.start()
        out_copies.extend([own, other])

    new_weights = [lambda j=j: new_weight(j) for j in range(NZ)]
    ag_hop(1, 4, new_weights)
    ag_hop(1, 5, new_weights)
    finish(2)
    finish(-2)
    finish(3)
    finish(-3)
    finish(4)

    for copy in out_copies:
        copy.wait()
    for j in range(NZ):
        m_copy(j).wait()
    for copy in pairs:
        copy.wait_send()
    for s in range(STEPS):
        for way in range(2):
            for h in range(1, 5 - way):
                for u in range(NSUB):
                    rs_copy(s, way, h, u).wait_send()
                    ag_copy(s, way, h, u).wait_send()
        for q in range(-4, 4):
            fw_copy(s, q).wait_send()
        for k in range(1, NZ):
            xr_copy(s, k).wait_send()
            sa_copy(s, k).wait_send()
        for k in range(1, 2 * NZ):
            rm_copy(s, k).wait_send()
        for k in range(1, n_rep):
            pl_copy(s, k).wait_send()
        sp_copy(s).wait_send()


def local(n_rep, inputs, targets, weight, momentum, indices):
    lanes = n_rep * 16
    arranged = indices.transpose(0, 1, 2, 4, 3).reshape(STEPS, n_rep * 8, 2 * NZ)
    any_space = pl.BlockSpec(memory_space=pl.ANY)
    dma = pltpu.SemaphoreType.DMA
    scratch = [
        pltpu.VMEM((STEPS, 2, TOK, ROWS), BF16),
        pltpu.VMEM((STEPS, ROWS, TOK), BF16),
        pltpu.VMEM((STEPS, TOK, BLOCK), BF16),
        pltpu.VMEM((NZ, 2 * ROWS, BLOCK), BF16),
        pltpu.VMEM((NZ, ROWS, 2 * BLOCK), F32),
        pltpu.VMEM((2, STEPS, n_rep * 8, 2 * NZ), jnp.int32),
        pltpu.VMEM((2, BLOCK, BLOCK), BF16),
        pltpu.VMEM((STEPS, NZ, lanes), F32),
        pltpu.VMEM((STEPS, 2, ROWS, BLOCK), BF16),
        pltpu.VMEM((STEPS, NZ, 32, ROWS), BF16),
        pltpu.VMEM((STEPS, NZ, 2 * ROWS, lanes), BF16),
        pltpu.VMEM((NZ, TOK, BLOCK), F32),
        pltpu.VMEM((STEPS, 2, TOK, BLOCK), BF16),
        pltpu.VMEM((STEPS, 7, TOK, BLOCK), BF16),
        pltpu.VMEM((STEPS, 2, NZ, TOK, BLOCK), BF16),
        pltpu.VMEM((BLOCK, ROWS), BF16),
        pltpu.VMEM((STEPS, NZ, 16, TOK), BF16),
        pltpu.VMEM((STEPS, NZ, 16, TOK), BF16),
        pltpu.VMEM((STEPS, NZ, 2, 8, BLOCK), F32),
        pltpu.VMEM((STEPS, 2 * NZ, 8, BLOCK), F32),
        pltpu.VMEM((STEPS, NZ, 16, BLOCK), BF16),
        pltpu.VMEM((STEPS, 2, NZ, 16, BLOCK), BF16),
        pltpu.VMEM((STEPS, n_rep, NZ, 16, BLOCK), BF16),
        dma((24,)), dma((11,)), dma((11,)),
        dma((STEPS, 7, NSUB)), dma((STEPS, 7, NSUB)), dma((STEPS, 7, NSUB)), dma((STEPS, 7, NSUB)),
        dma((STEPS, NZ)), dma((STEPS, NZ)), dma((STEPS, 2 * NZ)), dma((STEPS, 2 * NZ)),
        dma((STEPS, NZ)), dma((STEPS, NZ)), dma((STEPS,)), dma((STEPS,)),
        dma((STEPS, n_rep)), dma((STEPS, n_rep)), dma((STEPS, NZ + 1)), dma((STEPS, NZ + 1)),
        dma((2 * NZ,)), dma((NZ,)), dma((NZ,)),
    ]
    return pl.pallas_call(
        functools.partial(kernel, n_rep),
        out_shape=(
            jax.ShapeDtypeStruct(weight.shape, BF16),
            jax.ShapeDtypeStruct(momentum.shape, F32),
        ),
        in_specs=[pl.BlockSpec(memory_space=pltpu.HBM)] * 6,
        out_specs=(any_space, any_space),
        scratch_shapes=scratch,
        compiler_params=pltpu.CompilerParams(
            collective_id=0, has_side_effects=True, vmem_limit_bytes=40 << 20
        ),
    )(inputs, targets, weight, momentum, arranged, jnp.asarray(basis_parts()))


def solution(mesh):
    in_specs = (
        P(None, "rep", "tp"),
        P(None, "rep", "tp"),
        P("tp", None),
        P("rep", "tp", None),
        P(None, None, "tp", None, None),
    )
    out_specs = (P("tp", None), P("rep", "tp", None))
    return jax.shard_map(
        functools.partial(local, mesh.shape["rep"]), mesh=mesh, in_specs=in_specs, out_specs=out_specs, check_vma=False
    )
```

```python
import functools

import jax
import jax.numpy as jnp
import ml_dtypes
import numpy as np
from jax import lax
from jax.experimental import pallas as pl
from jax.experimental.pallas import tpu as pltpu
from jax.sharding import PartitionSpec as P

MESH = pl.DeviceIdType.MESH
BLOCK = 128
STEPS = 2
TOK = 512
NZ = 8
ROWS = 512
NSUB = 4
SIDE = 4
SUB = TOK // NSUB
F32 = jnp.float32
BF16 = jnp.bfloat16


def basis_parts():
    k = np.arange(BLOCK, dtype=np.float64)[:, None]
    n = np.arange(BLOCK, dtype=np.float64)[None, :]
    scale = np.where(k == 0, np.sqrt(1.0 / BLOCK), np.sqrt(2.0 / BLOCK))
    table = (scale * np.cos(np.pi * (2.0 * n + 1.0) * k / (2.0 * BLOCK))).T
    high = table.astype(ml_dtypes.bfloat16)
    low = (table - high.astype(np.float64)).astype(ml_dtypes.bfloat16)
    return np.stack([high, low])


def iota(shape, axis):
    return lax.broadcasted_iota(jnp.int32, shape, axis)


def kernel(
    n_rep,
    x_ref, t_ref, w_ref, m_ref, idx_ref, bt_ref,
    w_out, m_out,
    xa, xt, tv, wb, mb, iv, bt, frow, left, prow, lu,
    yp, ys, rl, ef, lx, xr_send, xr_land, rm_send, rm_land, s_send, sn, sall,
    load_sem, pair_send, pair_recv, rs_send, rs_recv, ag_send, ag_recv,
    xr_ssem, xr_rsem, rm_ssem, rm_rsem, sa_ssem, sa_rsem, sp_ssem, sp_rsem,
    pl_ssem, pl_rsem, fw_ssem, fw_rsem, out_sem, outp_ssem, outp_rsem, token,
):
    r = lax.axis_index("rep")
    me = lax.axis_index("tp")
    z = me // 2
    c = me % 2
    o = 1 - c
    lanes = n_rep * 16
    d = 1 - 2 * c
    partner = {"tp": 2 * z + o}

    def zz(k):
        return lax.rem(z + k + 2 * NZ, NZ)

    long_to = {"tp": 2 * zz(d) + c}
    short_to = {"tp": 2 * zz(-d) + c}

    def remote(src, dst, s, v, dev):
        return pltpu.make_async_remote_copy(
            src_ref=src, dst_ref=dst, send_sem=s, recv_sem=v, device_id=dev, device_id_type=MESH
        )

    def cols(j, h):
        return pl.ds(pl.multiple_of((2 * j + h) * BLOCK, BLOCK), BLOCK)

    half_own = pl.ds(pl.multiple_of(c * ROWS, ROWS), ROWS)
    half_other = pl.ds(pl.multiple_of(o * ROWS, ROWS), ROWS)

    side = SIDE
    along_x = [{"rep": (r // side) * side + lax.rem(r + k, side)} for k in (1, side - 1)]
    along_y = [{"rep": lax.rem(r + k * side, n_rep)} for k in (1, side - 1)]
    along_z = [long_to, short_to]
    if n_rep != side * side:
        along_x, along_y = [], []
    barrier = pltpu.get_barrier_semaphore()
    for peer in [partner] + along_z + along_x + along_y:
        pl.semaphore_signal(barrier, inc=1, device_id=peer, device_id_type=MESH)

    def tell(k, peers):
        for peer in peers:
            pl.semaphore_signal(token.at[k], inc=1, device_id=peer, device_id_type=MESH)

    def told(k, peers):
        if peers:
            pl.semaphore_wait(token.at[k], len(peers))

    loads = {}

    def load(name, k, src, dst):
        copy = pltpu.make_async_copy(src, dst, load_sem.at[k])
        copy.start()
        loads[name] = copy

    steps_out = (4, -3, 3, -2, 2, -1, 1, 0)
    load("ix", 2, idx_ref, iv.at[c])
    load("bt", 1, bt_ref, bt)
    load("x0", 0, x_ref.at[0], xa.at[0, c])
    for i in range(NZ):
        j = zz(d * steps_out[i])
        load(("w", i), 8 + i, w_ref.at[:, cols(j, c)], wb.at[j, half_own])
    load("x1", 3, x_ref.at[1], xa.at[1, c])
    load("t", 4, t_ref, tv)
    for j in range(NZ):
        load(("m", j), 16 + j, m_ref.at[0, :, pl.ds(2 * BLOCK * j, 2 * BLOCK)], mb.at[j])

    def build_own(s, g):
        mine = iv[c, s, pl.ds(pl.multiple_of(8 * r, 8), 8)].astype(F32).astype(BF16)
        lane = iota((16, BLOCK), 1)
        to = jnp.where(iota((16, BLOCK), 0) == 8 * g + lane // 16, 1.0, 0.0).astype(BF16)
        wide = jnp.dot(mine, to, preferred_element_type=F32)
        flat = jnp.where(iota((8, BLOCK), 1) % 8 == iota((8, BLOCK), 0), wide, 0.0)
        row = jnp.sum(flat, axis=0, keepdims=True)
        lane = iota((BLOCK, BLOCK), 1)
        hit = iota((BLOCK, BLOCK), 0).astype(F32) == row
        even = (lane // 8) % 2 == 0
        high = jnp.where(hit & even, 1.0, 0.0).astype(BF16)
        low = jnp.where(hit & jnp.logical_not(even), 1.0, 0.0).astype(BF16)
        both = jnp.dot(bt[0], high, preferred_element_type=F32) + jnp.dot(bt[1], low, preferred_element_type=F32)
        turned = both.T
        for a in range(4):
            left[s, g, a * BLOCK:(a + 1) * BLOCK] = jnp.where((lane % 8) // 2 == a, both, 0.0).astype(BF16)
            rows = jnp.where((iota((BLOCK, BLOCK), 0) % 8) // 2 == a, turned, 0.0).astype(BF16)
            prow[s, 4 * g:4 * g + 4, :, a * BLOCK:(a + 1) * BLOCK] = rows.reshape(4, 32, BLOCK)

    def project(s, j):
        table = prow[s, j]
        values = mb[j]
        high = values.astype(BF16)
        low = (values - high.astype(F32)).astype(BF16)
        out = jnp.dot(table, high, preferred_element_type=F32) + jnp.dot(table, low, preferred_element_type=F32)
        rm_send[s, j, 0] = out[0:8, :BLOCK] + out[8:16, :BLOCK]
        rm_send[s, j, 1] = out[16:24, BLOCK:] + out[24:32, BLOCK:]

    def early():
        loads["bt"].wait()
        loads["ix"].wait()
        build_own(0, 0)
        build_own(0, 1)

    early()
    pl.semaphore_wait(barrier, 1 + len(along_z + along_x + along_y))
    tell(0, along_z)
    tell(3, along_x)

    pairs = []

    def pair(k, src, dst):
        copy = remote(src, dst, pair_send.at[k], pair_recv.at[k], partner)
        copy.start()
        pairs.append(copy)

    pair(9, idx_ref, iv.at[c])
    pair(0, x_ref.at[0], xa.at[0, c])
    for i in range(NZ):
        j = zz(-d * steps_out[i])
        pair(1 + i, w_ref.at[:, cols(j, o)], wb.at[j, half_own])
    pair(10, x_ref.at[1], xa.at[1, c])

    order = [(zz(4 * d), zz(-3 * d)), (zz(3 * d), zz(-2 * d)), (zz(2 * d), zz(-d)), (zz(d), z)]

    def forward(s, k):
        p, q = order[k]
        for i in range(2):
            rows = pl.ds(i * 256, 256)
            acc = jnp.zeros((256, 2 * BLOCK), F32)
            for h in range(2):
                w = jnp.concatenate([wb[p, h * ROWS:(h + 1) * ROWS], wb[q, h * ROWS:(h + 1) * ROWS]], axis=1)
                acc += jnp.dot(xa[s, h, rows], w, preferred_element_type=F32)
            yp[2 * k, rows] = acc[:, :BLOCK]
            yp[2 * k + 1, rows] = acc[:, BLOCK:]
            if k == 0:
                ys[s, 0, rows] = acc[:, :BLOCK].astype(BF16)
                ys[s, 1, rows] = acc[:, BLOCK:].astype(BF16)

    def rs_copy(s, way, h, u):
        slot = h - 1 if way == 0 else 3 + h
        rows = pl.ds(u * SUB, SUB)
        if h == 1:
            src = ys.at[s, way, rows]
        else:
            src = rl.at[s, slot - 1, rows]
        return remote(src, rl.at[s, slot, rows], rs_send.at[s, slot, u], rs_recv.at[s, slot, u], (long_to, short_to)[way])

    def rs_first(s):
        for u in range(NSUB):
            for way in range(2):
                rs_copy(s, way, 1, u).start()

    def rs_wave(s, h, u):
        rows = pl.ds(u * SUB, SUB)
        for way in range(2):
            if h > 4 - way:
                continue
            rs_copy(s, way, h - 1, u).wait_recv()
            slot = h - 2 if way == 0 else 2 + h
            rl[s, slot, rows] = (rl[s, slot, rows].astype(F32) + yp[2 * (h - 1) + way, rows]).astype(BF16)
            rs_copy(s, way, h, u).start()

    def rs_last(s, u):
        rows = pl.ds(u * SUB, SUB)
        rs_copy(s, 1, 3, u).wait_recv()
        rs_copy(s, 0, 4, u).wait_recv()
        total = yp[7, rows] + rl[s, 3, rows].astype(F32) + rl[s, 6, rows].astype(F32)
        ef[s, c, z, rows] = (total - tv[s, rows].astype(F32)).astype(BF16)

    def rs_rest(s, work):
        for h in range(2, 5):
            for u in range(NSUB):
                rs_wave(s, h, u)
                run(work, (len(work) + NSUB * (5 - h) - u - 1) // (NSUB * (5 - h) - u))
        for u in range(NSUB):
            rs_last(s, u)
            if u < NSUB - 1:
                ag_wave(s, 1, u)

    def ag_copy(s, way, h, u):
        slot = h - 1 if way == 0 else 3 + h
        rows = pl.ds(u * SUB, SUB)
        origin = zz(-d * (h - 1)) if way == 0 else zz(d * (h - 1))
        block = ef.at[s, c, origin, rows]
        return remote(block, block, ag_send.at[s, slot, u], ag_recv.at[s, slot, u], (long_to, short_to)[way])

    def fw_copy(s, q):
        block = ef.at[s, c, zz(d * q)]
        k = q + 4 if q > -4 else 8
        return remote(block, block, fw_ssem.at[s, k], fw_rsem.at[s, k], partner)

    def fw_arrival(s, q):
        block = ef.at[s, o, zz(d * q)]
        k = 4 - q if q < 4 else 8
        return remote(block, block, fw_ssem.at[s, k], fw_rsem.at[s, k], partner)

    def ag_wave(s, h, u):
        for way in range(2):
            if h > 1 and h <= 5 - way:
                ag_copy(s, way, h - 1, u).wait_recv()
            if h <= 4 - way:
                ag_copy(s, way, h, u).start()
        if u == NSUB - 1:
            if h == 1:
                fw_copy(s, 0).start()
            else:
                fw_copy(s, 1 - h).start()
                if h <= 4:
                    fw_copy(s, h - 1).start()

    def ag_hop(s, h, work=(), low=0, high=NSUB):
        for u in range(low, high):
            ag_wave(s, h, u)
            run(work, (len(work) + high - u - 1) // (high - u))

    def arrange(s):
        pick = jnp.where(iota((NZ, 16), 1) == 2 * iota((NZ, 16), 0) + c, 1.0, 0.0).astype(BF16)
        half = n_rep * 8
        source = iota((half, lanes), 0)
        place = iota((half, lanes), 1)
        total = jnp.zeros((NZ, lanes), F32)
        for h in range(2):
            turned = lax.dot_general(
                pick, iv[h, s].astype(F32).astype(BF16), (((1,), (1,)), ((), ())), preferred_element_type=F32
            )
            to = jnp.where(place == (source // 8) * 16 + h * 8 + source % 8, 1.0, 0.0).astype(BF16)
            total += jnp.dot(turned.astype(BF16), to, preferred_element_type=F32)
        frow[s] = total

    def build_replicas(s, j):
        onehot = jnp.where(iota((BLOCK, lanes), 0).astype(F32) == frow[s, pl.ds(j, 1)], 1.0, 0.0).astype(BF16)
        kept = jnp.dot(bt[0], onehot, preferred_element_type=F32)
        for a in range(8):
            mine = (iota((BLOCK, lanes), 1) % 16) // 2 == a
            lu[s, j, a * BLOCK:(a + 1) * BLOCK] = jnp.where(mine, kept, 0.0).astype(BF16)

    def build_rows(s):
        lane = iota((lanes, BLOCK), 1)
        own = jnp.where(iota((lanes, BLOCK), 0) == 16 * r + lane % 16, 1.0, 0.0).astype(BF16)
        spread_rows = jnp.dot(frow[s].astype(BF16), own, preferred_element_type=F32)
        flat = jnp.where(iota((NZ, BLOCK), 1) // 16 == iota((NZ, BLOCK), 0), spread_rows, 0.0)
        row = jnp.sum(flat, axis=0, keepdims=True)
        onehot = jnp.where(iota((BLOCK, BLOCK), 0).astype(F32) == row, 1.0, 0.0).astype(BF16)
        kept = jnp.dot(bt[0], onehot, preferred_element_type=F32).T
        out = jnp.zeros((NZ * 16, TOK), F32)
        for h in range(2):
            for a in range(4):
                mine = (iota((BLOCK, BLOCK), 0) % 16) // 2 == 4 * h + a
                lx[:, a * BLOCK:(a + 1) * BLOCK] = jnp.where(mine, kept, 0.0).astype(BF16)
            out += lax.dot_general(lx[...], xa[s, h], (((1,), (1,)), ((), ())), preferred_element_type=F32)
        xr_send[s] = out.astype(BF16).reshape(NZ, 16, TOK)

    def xr_copy(s, k):
        to = zz(k)
        return remote(
            xr_send.at[s, to], xr_land.at[s, z], xr_ssem.at[s, k], xr_rsem.at[s, k], {"tp": 2 * to + c}
        )

    def rm_copy(s, k):
        to = lax.rem(me + k, 2 * NZ)
        return remote(
            rm_send.at[s, to // 2, to % 2], rm_land.at[s, me], rm_ssem.at[s, k], rm_rsem.at[s, k], {"tp": to}
        )

    def kept_rows(s):
        for k in range(1, NZ):
            xr_copy(s, k).wait_recv()
        for k in range(1, 2 * NZ):
            rm_copy(s, k).wait_recv()
        xr_land[s, z] = xr_send[s, z]
        rm_land[s, me] = rm_send[s, z, c]
        table = xr_land[s].reshape(NZ * 16, TOK)
        out = jnp.dot(table, ef[s, c, z], preferred_element_type=F32) * (1.0 / TOK)
        out += 0.9 * rm_land[s].reshape(NZ * 16, BLOCK)
        s_send[s] = out.astype(BF16).reshape(NZ, 16, BLOCK)

    def sa_copy(s, k):
        to = zz(k)
        return remote(
            s_send.at[s, to], sn.at[s, c, z], sa_ssem.at[s, k], sa_rsem.at[s, k], {"tp": 2 * to + c}
        )

    def sp_copy(s):
        return remote(sn.at[s, c], sn.at[s, c], sp_ssem.at[s], sp_rsem.at[s], partner)

    def pl_copy(s, k):
        return remote(
            sn.at[s, c], sall.at[s, r], pl_ssem.at[s, k], pl_rsem.at[s, k], {"rep": lax.rem(r + k, n_rep)}
        )

    def share(s):
        for k in range(1, NZ):
            sa_copy(s, k).start()
        sn[s, c, z] = s_send[s, z]

    def spread(s):
        for k in range(1, NZ):
            sa_copy(s, k).wait_recv()
        for k in range(1, n_rep):
            pl_copy(s, k).start()
        sp_copy(s).start()
        sall[s, r] = sn[s, c]

    def collect(s):
        for k in range(1, n_rep):
            pl_copy(s, k).wait_recv()

    def update(s, j):
        stack = sall[s, :, j].reshape(lanes, BLOCK)
        for i in range(4):
            rows = pl.ds(i * 256, 256)
            change = jnp.dot(lu[s, j, rows], stack, preferred_element_type=F32)
            wb[j, rows] = (wb[j, rows].astype(F32) - 0.1 * change).astype(BF16)

    def momentum(s, q):
        fw_arrival(s, q).wait_recv()
        j = zz(d * q)
        e = jnp.concatenate([ef[s, 0, j], ef[s, 1, j]], axis=1)
        parts = []
        for h in range(2):
            both = sn[s, h, j].astype(F32)
            parts.append(jnp.where(c == 0, both[:8], both[8:]))
        zero = jnp.zeros((8, BLOCK), F32)
        top = jnp.concatenate([parts[0], zero], axis=1)
        low = jnp.concatenate([zero, parts[1]], axis=1)
        block = jnp.concatenate([top, top, low, low], axis=0)
        right = jnp.concatenate([jnp.where(j % 4 == i, block, 0.0) for i in range(4)], axis=0).astype(BF16)
        for i in range(2):
            rows = pl.ds(i * 256, 256)
            grad = jnp.dot(xt[s, rows], e, preferred_element_type=F32)
            taken = jnp.dot(left[s, j // 4, rows], right, preferred_element_type=F32)
            mb[j, rows] = 0.9 * mb[j, rows] + grad * (1.0 / TOK) - taken

    def gain(q):
        momentum(0, q)
        project(1, zz(d * q))

    def finish(q):
        momentum(1, q)
        j = zz(d * q)
        m_copy(j).start()

    def m_copy(j):
        columns = pl.ds(pl.multiple_of(2 * BLOCK * j, 2 * BLOCK), 2 * BLOCK)
        return pltpu.make_async_copy(mb.at[j], m_out.at[0, :, columns], out_sem.at[NZ + j])

    def run(work, count):
        for _ in range(min(count, len(work))):
            work.pop(0)()

    def turn(s):
        xt[s] = xa[s, c].T

    loads["x0"].wait()
    pairs[1].wait_recv()

    def ready(k):
        for i in (2 * k, 2 * k + 1):
            loads["w", i].wait()
            pairs[2 + i].wait_recv()

    ready(0)
    forward(0, 0)
    rs_first(0)
    ready(1)
    forward(0, 1)
    pairs[0].wait_recv()
    told(0, along_z)
    tell(1, along_z)
    arrange(0)
    build_rows(0)
    told(1, along_z)
    tell(2, along_z)
    ready(2)
    ready(3)

    def send_rows():
        told(2, along_z)
        for k in range(1, NZ):
            xr_copy(0, k).start()

    def pass_on(k, before, after):
        def act():
            told(k, before)
            tell(k + 1, after)

        return act

    def send_products(s):
        for k in range(1, 2 * NZ):
            rm_copy(s, k).start()

    def second_rows():
        loads["x1"].wait()
        pairs[10].wait_recv()
        arrange(1)
        build_rows(1)

    def two(f, s, j):
        return lambda: (f(s, j), f(s, j + 1))

    def products(first):
        def some():
            for j in (first, first + 1):
                loads["m", j].wait()
                project(0, j)

        return some

    rs_rest(0, [
        lambda: forward(0, 2),
        lambda: (products(0)(), send_rows()),
        lambda: (products(2)(), pass_on(3, along_x, along_y)()),
        lambda: forward(0, 3),
        products(4),
        products(6),
        lambda: (send_products(0), loads["t"].wait()),
        lambda: turn(0),
        lambda: (two(build_replicas, 0, 0)(), pass_on(4, along_y, along_y)()),
        two(build_replicas, 0, 2),
        two(build_replicas, 0, 4),
        lambda: (two(build_replicas, 0, 6)(), told(5, along_y)),
    ])
    kept_rows(0)
    share(0)
    ag_wave(0, 1, NSUB - 1)
    second_rows()
    ag_hop(0, 2, (), 0, NSUB // 2)
    spread(0)
    ag_hop(0, 2, (), NSUB // 2, NSUB)
    for k in range(1, NZ):
        xr_copy(1, k).start()
    build_own(1, 0)
    build_own(1, 1)
    sp_copy(0).wait_recv()
    gain(0)
    ag_hop(0, 3)
    collect(0)

    for k in range(4):
        update(0, order[k][0])
        update(0, order[k][1])
        forward(1, k)
        if k == 0:
            rs_first(1)
        if k == 1:
            ag_hop(0, 4)

    def last_gain():
        gain(4)
        send_products(1)

    rs_rest(1, [
        lambda: gain(1),
        lambda: gain(-1),
        lambda: gain(2),
        lambda: gain(-2),
        lambda: (ag_hop(0, 5), gain(3)),
        lambda: gain(-3),
        last_gain,
        lambda: turn(1),
        two(build_replicas, 1, 0),
        two(build_replicas, 1, 2),
        two(build_replicas, 1, 4),
        two(build_replicas, 1, 6),
    ])
    kept_rows(1)
    share(1)
    ag_wave(1, 1, NSUB - 1)
    ag_hop(1, 2, (), 0, NSUB // 2)
    spread(1)
    ag_hop(1, 2, (), NSUB // 2, NSUB)
    sp_copy(1).wait_recv()
    ag_hop(1, 3, [lambda: finish(0), lambda: finish(1), lambda: finish(-1)])
    collect(1)
    out_copies = []

    def new_weight(j):
        update(1, j)
        own = pltpu.make_async_copy(wb.at[j, half_own], w_out.at[:, cols(j, c)], out_sem.at[j])
        own.start()
        other = remote(wb.at[j, half_other], w_out.at[:, cols(j, c)], outp_ssem.at[j], outp_rsem.at[j], partner)
        other.start()
        out_copies.extend([own, other])

    new_weights = [lambda j=j: new_weight(j) for j in range(NZ)]
    ag_hop(1, 4, new_weights[:4])
    ag_hop(1, 5, new_weights[4:])
    finish(2)
    finish(-2)
    finish(3)
    finish(-3)
    finish(4)

    for copy in out_copies:
        copy.wait()
    for j in range(NZ):
        m_copy(j).wait()
    for copy in pairs:
        copy.wait_send()
    for s in range(STEPS):
        for way in range(2):
            for h in range(1, 5 - way):
                for u in range(NSUB):
                    rs_copy(s, way, h, u).wait_send()
                    ag_copy(s, way, h, u).wait_send()
        for q in range(-4, 4):
            fw_copy(s, q).wait_send()
        for k in range(1, NZ):
            xr_copy(s, k).wait_send()
            sa_copy(s, k).wait_send()
        for k in range(1, 2 * NZ):
            rm_copy(s, k).wait_send()
        for k in range(1, n_rep):
            pl_copy(s, k).wait_send()
        sp_copy(s).wait_send()


def local(n_rep, inputs, targets, weight, momentum, indices):
    lanes = n_rep * 16
    arranged = indices.transpose(0, 1, 2, 4, 3).reshape(STEPS, n_rep * 8, 2 * NZ)
    any_space = pl.BlockSpec(memory_space=pl.ANY)
    dma = pltpu.SemaphoreType.DMA
    scratch = [
        pltpu.VMEM((STEPS, 2, TOK, ROWS), BF16),
        pltpu.VMEM((STEPS, ROWS, TOK), BF16),
        pltpu.VMEM((STEPS, TOK, BLOCK), BF16),
        pltpu.VMEM((NZ, 2 * ROWS, BLOCK), BF16),
        pltpu.VMEM((NZ, ROWS, 2 * BLOCK), F32),
        pltpu.VMEM((2, STEPS, n_rep * 8, 2 * NZ), jnp.int32),
        pltpu.VMEM((2, BLOCK, BLOCK), BF16),
        pltpu.VMEM((STEPS, NZ, lanes), F32),
        pltpu.VMEM((STEPS, 2, ROWS, BLOCK), BF16),
        pltpu.VMEM((STEPS, NZ, 32, ROWS), BF16),
        pltpu.VMEM((STEPS, NZ, 2 * ROWS, lanes), BF16),
        pltpu.VMEM((NZ, TOK, BLOCK), F32),
        pltpu.VMEM((STEPS, 2, TOK, BLOCK), BF16),
        pltpu.VMEM((STEPS, 7, TOK, BLOCK), BF16),
        pltpu.VMEM((STEPS, 2, NZ, TOK, BLOCK), BF16),
        pltpu.VMEM((BLOCK, ROWS), BF16),
        pltpu.VMEM((STEPS, NZ, 16, TOK), BF16),
        pltpu.VMEM((STEPS, NZ, 16, TOK), BF16),
        pltpu.VMEM((STEPS, NZ, 2, 8, BLOCK), F32),
        pltpu.VMEM((STEPS, 2 * NZ, 8, BLOCK), F32),
        pltpu.VMEM((STEPS, NZ, 16, BLOCK), BF16),
        pltpu.VMEM((STEPS, 2, NZ, 16, BLOCK), BF16),
        pltpu.VMEM((STEPS, n_rep, NZ, 16, BLOCK), BF16),
        dma((24,)), dma((11,)), dma((11,)),
        dma((STEPS, 7, NSUB)), dma((STEPS, 7, NSUB)), dma((STEPS, 7, NSUB)), dma((STEPS, 7, NSUB)),
        dma((STEPS, NZ)), dma((STEPS, NZ)), dma((STEPS, 2 * NZ)), dma((STEPS, 2 * NZ)),
        dma((STEPS, NZ)), dma((STEPS, NZ)), dma((STEPS,)), dma((STEPS,)),
        dma((STEPS, n_rep)), dma((STEPS, n_rep)), dma((STEPS, NZ + 1)), dma((STEPS, NZ + 1)),
        dma((2 * NZ,)), dma((NZ,)), dma((NZ,)),
        pltpu.SemaphoreType.REGULAR((6,)),
    ]
    return pl.pallas_call(
        functools.partial(kernel, n_rep),
        out_shape=(
            jax.ShapeDtypeStruct(weight.shape, BF16),
            jax.ShapeDtypeStruct(momentum.shape, F32),
        ),
        in_specs=[pl.BlockSpec(memory_space=pltpu.HBM)] * 6,
        out_specs=(any_space, any_space),
        scratch_shapes=scratch,
        compiler_params=pltpu.CompilerParams(
            collective_id=0, has_side_effects=True, vmem_limit_bytes=40 << 20
        ),
    )(*[pltpu.with_memory_space_constraint(v, pltpu.HBM) for v in (inputs, targets, weight, momentum, arranged, jnp.asarray(basis_parts()))])


def solution(mesh):
    in_specs = (
        P(None, "rep", "tp"),
        P(None, "rep", "tp"),
        P("tp", None),
        P("rep", "tp", None),
        P(None, None, "tp", None, None),
    )
    out_specs = (P("tp", None), P("rep", "tp", None))
    return jax.shard_map(
        functools.partial(local, mesh.shape["rep"]), mesh=mesh, in_specs=in_specs, out_specs=out_specs, check_vma=False
    )
```

```python
import functools

import jax
import jax.numpy as jnp
import ml_dtypes
import numpy as np
from jax import lax
from jax.experimental import pallas as pl
from jax.experimental.pallas import tpu as pltpu
from jax.sharding import PartitionSpec as P

MESH = pl.DeviceIdType.MESH
BLOCK = 128
STEPS = 2
TOK = 512
NZ = 8
ROWS = 512
NSUB = 4
SIDE = 4
SUB = TOK // NSUB
F32 = jnp.float32
BF16 = jnp.bfloat16


def basis_parts():
    k = np.arange(BLOCK, dtype=np.float64)[:, None]
    n = np.arange(BLOCK, dtype=np.float64)[None, :]
    scale = np.where(k == 0, np.sqrt(1.0 / BLOCK), np.sqrt(2.0 / BLOCK))
    table = (scale * np.cos(np.pi * (2.0 * n + 1.0) * k / (2.0 * BLOCK))).T
    high = table.astype(ml_dtypes.bfloat16)
    low = (table - high.astype(np.float64)).astype(ml_dtypes.bfloat16)
    return np.stack([high, low])


def iota(shape, axis):
    return lax.broadcasted_iota(jnp.int32, shape, axis)


def kernel(
    n_rep,
    x_ref, t_ref, w_ref, m_ref, idx_ref, bt_ref,
    w_out, m_out,
    xa, xt, tv, wb, mb, iv, bt, frow, left, prow, lu,
    yp, ys, rl, ef, lx, xr_send, xr_land, rm_send, rm_land, s_send, sn, sall,
    load_sem, pair_send, pair_recv, rs_send, rs_recv, ag_send, ag_recv,
    xr_ssem, xr_rsem, rm_ssem, rm_rsem, sa_ssem, sa_rsem, sp_ssem, sp_rsem,
    pl_ssem, pl_rsem, fw_ssem, fw_rsem, out_sem, outp_ssem, outp_rsem, token,
):
    r = lax.axis_index("rep")
    me = lax.axis_index("tp")
    z = me // 2
    c = me % 2
    o = 1 - c
    lanes = n_rep * 16
    d = 1 - 2 * c
    partner = {"tp": 2 * z + o}

    def zz(k):
        return lax.rem(z + k + 2 * NZ, NZ)

    long_to = {"tp": 2 * zz(d) + c}
    short_to = {"tp": 2 * zz(-d) + c}

    def remote(src, dst, s, v, dev):
        return pltpu.make_async_remote_copy(
            src_ref=src, dst_ref=dst, send_sem=s, recv_sem=v, device_id=dev, device_id_type=MESH
        )

    def cols(j, h):
        return pl.ds(pl.multiple_of((2 * j + h) * BLOCK, BLOCK), BLOCK)

    half_own = pl.ds(pl.multiple_of(c * ROWS, ROWS), ROWS)
    half_other = pl.ds(pl.multiple_of(o * ROWS, ROWS), ROWS)

    side = SIDE
    along_x = [{"rep": (r // side) * side + lax.rem(r + k, side)} for k in (1, side - 1)]
    along_y = [{"rep": lax.rem(r + k * side, n_rep)} for k in (1, side - 1)]
    along_z = [long_to, short_to]
    two_on = [{"tp": 2 * zz(2) + c}, {"tp": 2 * zz(-2) + c}]
    if n_rep != side * side:
        along_x, along_y = [], []
    barrier = pltpu.get_barrier_semaphore()
    for peer in [partner] + along_z + along_x + along_y:
        pl.semaphore_signal(barrier, inc=1, device_id=peer, device_id_type=MESH)

    def tell(k, peers):
        for peer in peers:
            pl.semaphore_signal(token.at[k], inc=1, device_id=peer, device_id_type=MESH)

    def told(k, peers):
        if peers:
            pl.semaphore_wait(token.at[k], len(peers))

    loads = {}

    def load(name, k, src, dst):
        copy = pltpu.make_async_copy(src, dst, load_sem.at[k])
        copy.start()
        loads[name] = copy

    steps_out = (4, -3, 3, -2, 2, -1, 1, 0)
    load("ix", 2, idx_ref, iv.at[c])
    load("bt", 1, bt_ref, bt)
    load("x0", 0, x_ref.at[0], xa.at[0, c])
    for i in range(NZ):
        j = zz(d * steps_out[i])
        load(("w", i), 8 + i, w_ref.at[:, cols(j, c)], wb.at[j, half_own])
    load("x1", 3, x_ref.at[1], xa.at[1, c])
    load("t", 4, t_ref, tv)
    for j in range(NZ):
        load(("m", j), 16 + j, m_ref.at[0, :, pl.ds(2 * BLOCK * j, 2 * BLOCK)], mb.at[j])

    def build_own(s, g):
        mine = iv[c, s, pl.ds(pl.multiple_of(8 * r, 8), 8)].astype(F32).astype(BF16)
        lane = iota((16, BLOCK), 1)
        to = jnp.where(iota((16, BLOCK), 0) == 8 * g + lane // 16, 1.0, 0.0).astype(BF16)
        wide = jnp.dot(mine, to, preferred_element_type=F32)
        flat = jnp.where(iota((8, BLOCK), 1) % 8 == iota((8, BLOCK), 0), wide, 0.0)
        row = jnp.sum(flat, axis=0, keepdims=True)
        lane = iota((BLOCK, BLOCK), 1)
        hit = iota((BLOCK, BLOCK), 0).astype(F32) == row
        even = (lane // 8) % 2 == 0
        high = jnp.where(hit & even, 1.0, 0.0).astype(BF16)
        low = jnp.where(hit & jnp.logical_not(even), 1.0, 0.0).astype(BF16)
        both = jnp.dot(bt[0], high, preferred_element_type=F32) + jnp.dot(bt[1], low, preferred_element_type=F32)
        turned = both.T
        for a in range(4):
            left[s, g, a * BLOCK:(a + 1) * BLOCK] = jnp.where((lane % 8) // 2 == a, both, 0.0).astype(BF16)
            rows = jnp.where((iota((BLOCK, BLOCK), 0) % 8) // 2 == a, turned, 0.0).astype(BF16)
            prow[s, 4 * g:4 * g + 4, :, a * BLOCK:(a + 1) * BLOCK] = rows.reshape(4, 32, BLOCK)

    def project(s, j):
        table = prow[s, j]
        values = mb[j]
        high = values.astype(BF16)
        low = (values - high.astype(F32)).astype(BF16)
        out = jnp.dot(table, high, preferred_element_type=F32) + jnp.dot(table, low, preferred_element_type=F32)
        rm_send[s, 0, j] = out[0:8, :BLOCK] + out[8:16, :BLOCK]
        rm_send[s, 1, j] = out[16:24, BLOCK:] + out[24:32, BLOCK:]

    def early():
        loads["bt"].wait()
        loads["ix"].wait()
        build_own(0, 0)
        build_own(0, 1)

    early()
    pl.semaphore_wait(barrier, 1 + len(along_z + along_x + along_y))
    tell(0, along_z)
    tell(3, along_x)

    pairs = []

    def pair(k, src, dst):
        copy = remote(src, dst, pair_send.at[k], pair_recv.at[k], partner)
        copy.start()
        pairs.append(copy)

    pair(9, idx_ref, iv.at[c])
    pair(0, x_ref.at[0], xa.at[0, c])
    for i in range(NZ):
        j = zz(-d * steps_out[i])
        pair(1 + i, w_ref.at[:, cols(j, o)], wb.at[j, half_own])
    pair(10, x_ref.at[1], xa.at[1, c])

    order = [(zz(4 * d), zz(-3 * d)), (zz(3 * d), zz(-2 * d)), (zz(2 * d), zz(-d)), (zz(d), z)]

    def forward(s, k):
        p, q = order[k]
        for i in range(2):
            rows = pl.ds(i * 256, 256)
            acc = jnp.zeros((256, 2 * BLOCK), F32)
            for h in range(2):
                w = jnp.concatenate([wb[p, h * ROWS:(h + 1) * ROWS], wb[q, h * ROWS:(h + 1) * ROWS]], axis=1)
                acc += jnp.dot(xa[s, h, rows], w, preferred_element_type=F32)
            yp[2 * k, rows] = acc[:, :BLOCK]
            yp[2 * k + 1, rows] = acc[:, BLOCK:]
            if k == 0:
                ys[s, 0, rows] = acc[:, :BLOCK].astype(BF16)
                ys[s, 1, rows] = acc[:, BLOCK:].astype(BF16)
                for u in range(i * NSUB // 2, (i + 1) * NSUB // 2):
                    for way in range(2):
                        rs_copy(s, way, 1, u).start()

    def rs_copy(s, way, h, u):
        slot = h - 1 if way == 0 else 3 + h
        rows = pl.ds(u * SUB, SUB)
        if h == 1:
            src = ys.at[s, way, rows]
        else:
            src = rl.at[s, slot - 1, rows]
        return remote(src, rl.at[s, slot, rows], rs_send.at[s, slot, u], rs_recv.at[s, slot, u], (long_to, short_to)[way])

    def rs_wave(s, h, u):
        rows = pl.ds(u * SUB, SUB)
        for way in range(2):
            if h > 4 - way:
                continue
            rs_copy(s, way, h - 1, u).wait_recv()
            slot = h - 2 if way == 0 else 2 + h
            rl[s, slot, rows] = (rl[s, slot, rows].astype(F32) + yp[2 * (h - 1) + way, rows]).astype(BF16)
            rs_copy(s, way, h, u).start()

    def rs_last(s, u):
        rows = pl.ds(u * SUB, SUB)
        rs_copy(s, 1, 3, u).wait_recv()
        rs_copy(s, 0, 4, u).wait_recv()
        total = yp[7, rows] + rl[s, 3, rows].astype(F32) + rl[s, 6, rows].astype(F32)
        ef[s, c, z, rows] = (total - tv[s, rows].astype(F32)).astype(BF16)

    def rs_rest(s, work):
        for h in range(2, 5):
            for u in range(NSUB):
                rs_wave(s, h, u)
                run(work, (len(work) + NSUB * (5 - h) - u - 1) // (NSUB * (5 - h) - u))
        for u in range(NSUB):
            rs_last(s, u)
            if u < NSUB - 1:
                ag_wave(s, 1, u)

    def ag_copy(s, way, h, u):
        slot = h - 1 if way == 0 else 3 + h
        rows = pl.ds(u * SUB, SUB)
        origin = zz(-d * (h - 1)) if way == 0 else zz(d * (h - 1))
        block = ef.at[s, c, origin, rows]
        return remote(block, block, ag_send.at[s, slot, u], ag_recv.at[s, slot, u], (long_to, short_to)[way])

    def fw_copy(s, q):
        block = ef.at[s, c, zz(d * q)]
        k = q + 4 if q > -4 else 8
        return remote(block, block, fw_ssem.at[s, k], fw_rsem.at[s, k], partner)

    def fw_arrival(s, q):
        block = ef.at[s, o, zz(d * q)]
        k = 4 - q if q < 4 else 8
        return remote(block, block, fw_ssem.at[s, k], fw_rsem.at[s, k], partner)

    def ag_wave(s, h, u):
        for way in range(2):
            if h > 1 and h <= 5 - way:
                ag_copy(s, way, h - 1, u).wait_recv()
            if h <= 4 - way:
                ag_copy(s, way, h, u).start()
        if u == NSUB - 1:
            if h == 1:
                fw_copy(s, 0).start()
            else:
                fw_copy(s, 1 - h).start()
                if h <= 4:
                    fw_copy(s, h - 1).start()

    def ag_hop(s, h, work=(), low=0, high=NSUB):
        for u in range(low, high):
            ag_wave(s, h, u)
            run(work, (len(work) + high - u - 1) // (high - u))

    def arrange(s):
        pick = jnp.where(iota((NZ, 16), 1) == 2 * iota((NZ, 16), 0) + c, 1.0, 0.0).astype(BF16)
        half = n_rep * 8
        source = iota((half, lanes), 0)
        place = iota((half, lanes), 1)
        total = jnp.zeros((NZ, lanes), F32)
        for h in range(2):
            turned = lax.dot_general(
                pick, iv[h, s].astype(F32).astype(BF16), (((1,), (1,)), ((), ())), preferred_element_type=F32
            )
            to = jnp.where(place == (source // 8) * 16 + h * 8 + source % 8, 1.0, 0.0).astype(BF16)
            total += jnp.dot(turned.astype(BF16), to, preferred_element_type=F32)
        frow[s] = total

    def build_replicas(s, j):
        onehot = jnp.where(iota((BLOCK, lanes), 0).astype(F32) == frow[s, pl.ds(j, 1)], 1.0, 0.0).astype(BF16)
        kept = jnp.dot(bt[0], onehot, preferred_element_type=F32)
        for a in range(8):
            mine = (iota((BLOCK, lanes), 1) % 16) // 2 == a
            lu[s, j, a * BLOCK:(a + 1) * BLOCK] = jnp.where(mine, kept, 0.0).astype(BF16)

    def build_rows(s):
        lane = iota((lanes, BLOCK), 1)
        own = jnp.where(iota((lanes, BLOCK), 0) == 16 * r + lane % 16, 1.0, 0.0).astype(BF16)
        spread_rows = jnp.dot(frow[s].astype(BF16), own, preferred_element_type=F32)
        flat = jnp.where(iota((NZ, BLOCK), 1) // 16 == iota((NZ, BLOCK), 0), spread_rows, 0.0)
        row = jnp.sum(flat, axis=0, keepdims=True)
        onehot = jnp.where(iota((BLOCK, BLOCK), 0).astype(F32) == row, 1.0, 0.0).astype(BF16)
        kept = jnp.dot(bt[0], onehot, preferred_element_type=F32).T
        out = jnp.zeros((NZ * 16, TOK), F32)
        for h in range(2):
            for a in range(4):
                mine = (iota((BLOCK, BLOCK), 0) % 16) // 2 == 4 * h + a
                lx[:, a * BLOCK:(a + 1) * BLOCK] = jnp.where(mine, kept, 0.0).astype(BF16)
            out += lax.dot_general(lx[...], xa[s, h], (((1,), (1,)), ((), ())), preferred_element_type=F32)
        xr_send[s] = out.astype(BF16).reshape(NZ, 16, TOK)

    def xr_copy(s, k):
        to = zz(k)
        return remote(
            xr_send.at[s, to], xr_land.at[s, z], xr_ssem.at[s, k], xr_rsem.at[s, k], {"tp": 2 * to + c}
        )

    def rm_copy(s):
        return remote(rm_send.at[s, o], rm_land.at[s], rm_ssem.at[s], rm_rsem.at[s], partner)

    def kept_rows(s):
        for k in range(1, NZ):
            xr_copy(s, k).wait_recv()
        xr_land[s, z] = xr_send[s, z]
        table = xr_land[s].reshape(NZ * 16, TOK)
        out = jnp.dot(table, ef[s, c, z], preferred_element_type=F32) * (1.0 / TOK)
        s_send[s] = out.astype(BF16).reshape(NZ, 16, BLOCK)

    def sa_copy(s, k):
        to = zz(k)
        return remote(
            s_send.at[s, to], sn.at[s, c, z], sa_ssem.at[s, k], sa_rsem.at[s, k], {"tp": 2 * to + c}
        )

    def sp_copy(s):
        return remote(sn.at[s, c], sn.at[s, c], sp_ssem.at[s], sp_rsem.at[s], partner)

    def pl_copy(s, k):
        return remote(
            sn.at[s, c], sall.at[s, r], pl_ssem.at[s, k], pl_rsem.at[s, k], {"rep": lax.rem(r + k, n_rep)}
        )

    def share(s):
        for k in range(1, NZ):
            sa_copy(s, k).start()
        sn[s, c, z] = s_send[s, z]

    def spread(s):
        for k in range(1, NZ):
            sa_copy(s, k).wait_recv()
        rm_copy(s).wait_recv()
        own, other = rm_send[s, c], rm_land[s]
        rows = jnp.concatenate([jnp.where(c == 0, own, other), jnp.where(c == 0, other, own)], axis=1)
        sn[s, c] = (sn[s, c].astype(F32) + 0.9 * rows).astype(BF16)
        for k in range(1, n_rep):
            pl_copy(s, k).start()
        sp_copy(s).start()
        sall[s, r] = sn[s, c]

    def collect(s):
        for k in range(1, n_rep):
            pl_copy(s, k).wait_recv()

    def update(s, j):
        stack = sall[s, :, j].reshape(lanes, BLOCK)
        for i in range(4):
            rows = pl.ds(i * 256, 256)
            change = jnp.dot(lu[s, j, rows], stack, preferred_element_type=F32)
            wb[j, rows] = (wb[j, rows].astype(F32) - 0.1 * change).astype(BF16)

    def momentum(s, q):
        fw_arrival(s, q).wait_recv()
        j = zz(d * q)
        e = jnp.concatenate([ef[s, 0, j], ef[s, 1, j]], axis=1)
        parts = []
        for h in range(2):
            both = sn[s, h, j].astype(F32)
            parts.append(jnp.where(c == 0, both[:8], both[8:]))
        zero = jnp.zeros((8, BLOCK), F32)
        top = jnp.concatenate([parts[0], zero], axis=1)
        low = jnp.concatenate([zero, parts[1]], axis=1)
        block = jnp.concatenate([top, top, low, low], axis=0)
        right = jnp.concatenate([jnp.where(j % 4 == i, block, 0.0) for i in range(4)], axis=0).astype(BF16)
        for i in range(2):
            rows = pl.ds(i * 256, 256)
            grad = jnp.dot(xt[s, rows], e, preferred_element_type=F32)
            taken = jnp.dot(left[s, j // 4, rows], right, preferred_element_type=F32)
            mb[j, rows] = 0.9 * mb[j, rows] + grad * (1.0 / TOK) - taken

    def gain(q):
        momentum(0, q)
        project(1, zz(d * q))

    def finish(q):
        momentum(1, q)
        j = zz(d * q)
        m_copy(j).start()

    def m_copy(j):
        columns = pl.ds(pl.multiple_of(2 * BLOCK * j, 2 * BLOCK), 2 * BLOCK)
        return pltpu.make_async_copy(mb.at[j], m_out.at[0, :, columns], out_sem.at[NZ + j])

    def run(work, count):
        for _ in range(min(count, len(work))):
            work.pop(0)()

    def turn(s):
        xt[s] = xa[s, c].T

    loads["x0"].wait()
    pairs[1].wait_recv()

    def ready(k):
        for i in (2 * k, 2 * k + 1):
            loads["w", i].wait()
            pairs[2 + i].wait_recv()

    ready(0)
    forward(0, 0)
    told(0, along_z)
    tell(1, two_on)
    ready(1)
    forward(0, 1)
    pairs[0].wait_recv()
    arrange(0)
    build_rows(0)
    ready(2)
    ready(3)
    told(1, two_on)
    for k in range(1, NZ):
        xr_copy(0, k).start()

    def pass_on(k, before, after):
        def act():
            told(k, before)
            tell(k + 1, after)

        return act

    def second_rows():
        loads["x1"].wait()
        pairs[10].wait_recv()
        arrange(1)
        build_rows(1)

    def two(f, s, j):
        return lambda: (f(s, j), f(s, j + 1))

    def products(first):
        def some():
            for j in (first, first + 1):
                loads["m", j].wait()
                project(0, j)

        return some

    rs_rest(0, [
        lambda: forward(0, 2),
        products(0),
        lambda: (products(2)(), pass_on(3, along_x, along_y)()),
        lambda: forward(0, 3),
        products(4),
        products(6),
        lambda: (rm_copy(0).start(), loads["t"].wait()),
        lambda: turn(0),
        second_rows,
        lambda: (two(build_replicas, 0, 0)(), pass_on(4, along_y, along_y)()),
        two(build_replicas, 0, 2),
        two(build_replicas, 0, 4),
        lambda: (two(build_replicas, 0, 6)(), told(5, along_y)),
    ])
    kept_rows(0)
    share(0)
    ag_wave(0, 1, NSUB - 1)
    ag_hop(0, 2, (), 0, NSUB // 2)
    spread(0)
    ag_hop(0, 2, (), NSUB // 2, NSUB)
    for k in range(1, NZ):
        xr_copy(1, k).start()
    build_own(1, 0)
    build_own(1, 1)
    sp_copy(0).wait_recv()
    gain(0)
    ag_hop(0, 3)
    collect(0)

    for k in range(4):
        update(0, order[k][0])
        update(0, order[k][1])
        forward(1, k)
        if k == 1:
            ag_hop(0, 4)

    def last_gain():
        gain(4)
        rm_copy(1).start()

    rs_rest(1, [
        lambda: gain(1),
        lambda: gain(-1),
        lambda: gain(2),
        lambda: gain(-2),
        lambda: (ag_hop(0, 5), gain(3)),
        lambda: gain(-3),
        last_gain,
        lambda: turn(1),
        two(build_replicas, 1, 0),
        two(build_replicas, 1, 2),
        two(build_replicas, 1, 4),
        two(build_replicas, 1, 6),
    ])
    kept_rows(1)
    share(1)
    ag_wave(1, 1, NSUB - 1)
    ag_hop(1, 2, (), 0, NSUB // 2)
    spread(1)
    ag_hop(1, 2, (), NSUB // 2, NSUB)
    sp_copy(1).wait_recv()
    ag_hop(1, 3, [lambda: finish(0), lambda: finish(1), lambda: finish(-1)])
    out_copies = []

    def new_weight(j):
        update(1, j)
        own = pltpu.make_async_copy(wb.at[j, half_own], w_out.at[:, cols(j, c)], out_sem.at[j])
        own.start()
        other = remote(wb.at[j, half_other], w_out.at[:, cols(j, c)], outp_ssem.at[j], outp_rsem.at[j], partner)
        other.start()
        out_copies.extend([own, other])

    ag_hop(1, 4, [lambda: finish(2), lambda: finish(-2)])
    collect(1)
    for j in range(NZ):
        new_weight(j)
    ag_hop(1, 5, [lambda: finish(3), lambda: finish(-3)])
    finish(4)

    for copy in out_copies:
        copy.wait()
    for j in range(NZ):
        m_copy(j).wait()
    for copy in pairs:
        copy.wait_send()
    for s in range(STEPS):
        for way in range(2):
            for h in range(1, 5 - way):
                for u in range(NSUB):
                    rs_copy(s, way, h, u).wait_send()
                    ag_copy(s, way, h, u).wait_send()
        for q in range(-4, 4):
            fw_copy(s, q).wait_send()
        for k in range(1, NZ):
            xr_copy(s, k).wait_send()
            sa_copy(s, k).wait_send()
        rm_copy(s).wait_send()
        for k in range(1, n_rep):
            pl_copy(s, k).wait_send()
        sp_copy(s).wait_send()


def local(n_rep, inputs, targets, weight, momentum, indices):
    lanes = n_rep * 16
    arranged = indices.transpose(0, 1, 2, 4, 3).reshape(STEPS, n_rep * 8, 2 * NZ)
    any_space = pl.BlockSpec(memory_space=pl.ANY)
    dma = pltpu.SemaphoreType.DMA
    scratch = [
        pltpu.VMEM((STEPS, 2, TOK, ROWS), BF16),
        pltpu.VMEM((STEPS, ROWS, TOK), BF16),
        pltpu.VMEM((STEPS, TOK, BLOCK), BF16),
        pltpu.VMEM((NZ, 2 * ROWS, BLOCK), BF16),
        pltpu.VMEM((NZ, ROWS, 2 * BLOCK), F32),
        pltpu.VMEM((2, STEPS, n_rep * 8, 2 * NZ), jnp.int32),
        pltpu.VMEM((2, BLOCK, BLOCK), BF16),
        pltpu.VMEM((STEPS, NZ, lanes), F32),
        pltpu.VMEM((STEPS, 2, ROWS, BLOCK), BF16),
        pltpu.VMEM((STEPS, NZ, 32, ROWS), BF16),
        pltpu.VMEM((STEPS, NZ, 2 * ROWS, lanes), BF16),
        pltpu.VMEM((NZ, TOK, BLOCK), F32),
        pltpu.VMEM((STEPS, 2, TOK, BLOCK), BF16),
        pltpu.VMEM((STEPS, 7, TOK, BLOCK), BF16),
        pltpu.VMEM((STEPS, 2, NZ, TOK, BLOCK), BF16),
        pltpu.VMEM((BLOCK, ROWS), BF16),
        pltpu.VMEM((STEPS, NZ, 16, TOK), BF16),
        pltpu.VMEM((STEPS, NZ, 16, TOK), BF16),
        pltpu.VMEM((STEPS, 2, NZ, 8, BLOCK), F32),
        pltpu.VMEM((STEPS, NZ, 8, BLOCK), F32),
        pltpu.VMEM((STEPS, NZ, 16, BLOCK), BF16),
        pltpu.VMEM((STEPS, 2, NZ, 16, BLOCK), BF16),
        pltpu.VMEM((STEPS, n_rep, NZ, 16, BLOCK), BF16),
        dma((24,)), dma((11,)), dma((11,)),
        dma((STEPS, 7, NSUB)), dma((STEPS, 7, NSUB)), dma((STEPS, 7, NSUB)), dma((STEPS, 7, NSUB)),
        dma((STEPS, NZ)), dma((STEPS, NZ)), dma((STEPS,)), dma((STEPS,)),
        dma((STEPS, NZ)), dma((STEPS, NZ)), dma((STEPS,)), dma((STEPS,)),
        dma((STEPS, n_rep)), dma((STEPS, n_rep)), dma((STEPS, NZ + 1)), dma((STEPS, NZ + 1)),
        dma((2 * NZ,)), dma((NZ,)), dma((NZ,)),
        pltpu.SemaphoreType.REGULAR((6,)),
    ]
    return pl.pallas_call(
        functools.partial(kernel, n_rep),
        out_shape=(
            jax.ShapeDtypeStruct(weight.shape, BF16),
            jax.ShapeDtypeStruct(momentum.shape, F32),
        ),
        in_specs=[pl.BlockSpec(memory_space=pltpu.HBM)] * 6,
        out_specs=(any_space, any_space),
        scratch_shapes=scratch,
        compiler_params=pltpu.CompilerParams(
            collective_id=0, has_side_effects=True, vmem_limit_bytes=40 << 20
        ),
    )(*[pltpu.with_memory_space_constraint(v, pltpu.HBM) for v in (inputs, targets, weight, momentum, arranged, jnp.asarray(basis_parts()))])


def solution(mesh):
    in_specs = (
        P(None, "rep", "tp"),
        P(None, "rep", "tp"),
        P("tp", None),
        P("rep", "tp", None),
        P(None, None, "tp", None, None),
    )
    out_specs = (P("tp", None), P("rep", "tp", None))
    return jax.shard_map(
        functools.partial(local, mesh.shape["rep"]), mesh=mesh, in_specs=in_specs, out_specs=out_specs, check_vma=False
    )
```

```python
import functools

import jax
import jax.numpy as jnp
import ml_dtypes
import numpy as np
from jax import lax
from jax.experimental import pallas as pl
from jax.experimental.pallas import tpu as pltpu
from jax.sharding import PartitionSpec as P

MESH = pl.DeviceIdType.MESH
BLOCK = 128
STEPS = 2
TOK = 512
NZ = 8
ROWS = 512
NSUB = 4
SIDE = 4
SUB = TOK // NSUB
F32 = jnp.float32
BF16 = jnp.bfloat16


def basis_parts():
    k = np.arange(BLOCK, dtype=np.float64)[:, None]
    n = np.arange(BLOCK, dtype=np.float64)[None, :]
    scale = np.where(k == 0, np.sqrt(1.0 / BLOCK), np.sqrt(2.0 / BLOCK))
    table = (scale * np.cos(np.pi * (2.0 * n + 1.0) * k / (2.0 * BLOCK))).T
    high = table.astype(ml_dtypes.bfloat16)
    low = (table - high.astype(np.float64)).astype(ml_dtypes.bfloat16)
    return np.stack([high, low])


def iota(shape, axis):
    return lax.broadcasted_iota(jnp.int32, shape, axis)


def kernel(
    n_rep,
    x_ref, t_ref, w_ref, m_ref, idx_ref, bt_ref,
    w_out, m_out,
    xa, xt, tv, wb, mb, iv, bt, frow, left, prow, lu,
    yp, ys, rl, ef, lx, xr_send, xr_land, rm_send, rm_land, s_send, sn, ps, sall,
    load_sem, pair_send, pair_recv, rs_send, rs_recv, ag_send, ag_recv,
    xr_ssem, xr_rsem, rm_ssem, rm_rsem, sa_ssem, sa_rsem, sp_ssem, sp_rsem,
    pl_ssem, pl_rsem, fw_ssem, fw_rsem, out_sem, outp_ssem, outp_rsem, token,
):
    r = lax.axis_index("rep")
    me = lax.axis_index("tp")
    z = me // 2
    c = me % 2
    o = 1 - c
    lanes = n_rep * 16
    d = 1 - 2 * c
    partner = {"tp": 2 * z + o}

    def zz(k):
        return lax.rem(z + k + 2 * NZ, NZ)

    long_to = {"tp": 2 * zz(d) + c}
    short_to = {"tp": 2 * zz(-d) + c}

    def remote(src, dst, s, v, dev):
        return pltpu.make_async_remote_copy(
            src_ref=src, dst_ref=dst, send_sem=s, recv_sem=v, device_id=dev, device_id_type=MESH
        )

    def cols(j, h):
        return pl.ds(pl.multiple_of((2 * j + h) * BLOCK, BLOCK), BLOCK)

    half_own = pl.ds(pl.multiple_of(c * ROWS, ROWS), ROWS)
    half_other = pl.ds(pl.multiple_of(o * ROWS, ROWS), ROWS)

    side = SIDE
    along_x = [{"rep": (r // side) * side + lax.rem(r + k, side)} for k in (1, side - 1)]
    along_y = [{"rep": lax.rem(r + k * side, n_rep)} for k in (1, side - 1)]
    along_z = [long_to, short_to]
    two_on = [{"tp": 2 * zz(2) + c}, {"tp": 2 * zz(-2) + c}]
    if n_rep != side * side:
        along_x, along_y = [], []
    barrier = pltpu.get_barrier_semaphore()
    for peer in [partner] + along_z + along_x + along_y:
        pl.semaphore_signal(barrier, inc=1, device_id=peer, device_id_type=MESH)

    def tell(k, peers):
        for peer in peers:
            pl.semaphore_signal(token.at[k], inc=1, device_id=peer, device_id_type=MESH)

    def told(k, peers):
        if peers:
            pl.semaphore_wait(token.at[k], len(peers))

    loads = {}

    def load(name, k, src, dst):
        copy = pltpu.make_async_copy(src, dst, load_sem.at[k])
        copy.start()
        loads[name] = copy

    steps_out = (4, -3, 3, -2, 2, -1, 1, 0)
    load("ix", 2, idx_ref, iv.at[c])
    load("bt", 1, bt_ref, bt)
    load("x0", 0, x_ref.at[0], xa.at[0, c])
    for i in range(NZ):
        j = zz(d * steps_out[i])
        load(("w", i), 8 + i, w_ref.at[:, cols(j, c)], wb.at[j, half_own])
    load("x1", 3, x_ref.at[1], xa.at[1, c])
    load("t", 4, t_ref, tv)
    for j in range(NZ):
        load(("m", j), 16 + j, m_ref.at[0, :, pl.ds(2 * BLOCK * j, 2 * BLOCK)], mb.at[j])

    def build_own(s, g):
        mine = iv[c, s, pl.ds(pl.multiple_of(8 * r, 8), 8)].astype(F32).astype(BF16)
        lane = iota((16, BLOCK), 1)
        to = jnp.where(iota((16, BLOCK), 0) == 8 * g + lane // 16, 1.0, 0.0).astype(BF16)
        wide = jnp.dot(mine, to, preferred_element_type=F32)
        flat = jnp.where(iota((8, BLOCK), 1) % 8 == iota((8, BLOCK), 0), wide, 0.0)
        row = jnp.sum(flat, axis=0, keepdims=True)
        lane = iota((BLOCK, BLOCK), 1)
        hit = iota((BLOCK, BLOCK), 0).astype(F32) == row
        even = (lane // 8) % 2 == 0
        high = jnp.where(hit & even, 1.0, 0.0).astype(BF16)
        low = jnp.where(hit & jnp.logical_not(even), 1.0, 0.0).astype(BF16)
        both = jnp.dot(bt[0], high, preferred_element_type=F32) + jnp.dot(bt[1], low, preferred_element_type=F32)
        turned = both.T
        for a in range(4):
            left[s, g, a * BLOCK:(a + 1) * BLOCK] = jnp.where((lane % 8) // 2 == a, both, 0.0).astype(BF16)
            rows = jnp.where((iota((BLOCK, BLOCK), 0) % 8) // 2 == a, turned, 0.0).astype(BF16)
            prow[s, 4 * g:4 * g + 4, :, a * BLOCK:(a + 1) * BLOCK] = rows.reshape(4, 32, BLOCK)

    def project(s, j):
        table = prow[s, j]
        values = mb[j]
        high = values.astype(BF16)
        low = (values - high.astype(F32)).astype(BF16)
        out = jnp.dot(table, high, preferred_element_type=F32) + jnp.dot(table, low, preferred_element_type=F32)
        rm_send[s, 0, j] = out[0:8, :BLOCK] + out[8:16, :BLOCK]
        rm_send[s, 1, j] = out[16:24, BLOCK:] + out[24:32, BLOCK:]

    def early():
        loads["bt"].wait()
        loads["ix"].wait()
        build_own(0, 0)
        build_own(0, 1)

    early()
    pl.semaphore_wait(barrier, 1 + len(along_z + along_x + along_y))
    tell(0, along_z)
    tell(3, along_x)

    pairs = []

    def pair(k, src, dst):
        copy = remote(src, dst, pair_send.at[k], pair_recv.at[k], partner)
        copy.start()
        pairs.append(copy)

    pair(9, idx_ref, iv.at[c])
    pair(0, x_ref.at[0], xa.at[0, c])
    for i in range(NZ):
        j = zz(-d * steps_out[i])
        pair(1 + i, w_ref.at[:, cols(j, o)], wb.at[j, half_own])
    pair(10, x_ref.at[1], xa.at[1, c])

    order = [(zz(4 * d), zz(-3 * d)), (zz(3 * d), zz(-2 * d)), (zz(2 * d), zz(-d)), (zz(d), z)]

    def forward(s, k):
        p, q = order[k]
        for i in range(2):
            rows = pl.ds(i * 256, 256)
            acc = jnp.zeros((256, 2 * BLOCK), F32)
            for h in range(2):
                w = jnp.concatenate([wb[p, h * ROWS:(h + 1) * ROWS], wb[q, h * ROWS:(h + 1) * ROWS]], axis=1)
                acc += jnp.dot(xa[s, h, rows], w, preferred_element_type=F32)
            yp[2 * k, rows] = acc[:, :BLOCK]
            yp[2 * k + 1, rows] = acc[:, BLOCK:]
            if k == 0:
                ys[s, 0, rows] = acc[:, :BLOCK].astype(BF16)
                ys[s, 1, rows] = acc[:, BLOCK:].astype(BF16)
                for u in range(i * NSUB // 2, (i + 1) * NSUB // 2):
                    for way in range(2):
                        rs_copy(s, way, 1, u).start()

    def rs_copy(s, way, h, u):
        slot = h - 1 if way == 0 else 3 + h
        rows = pl.ds(u * SUB, SUB)
        if h == 1:
            src = ys.at[s, way, rows]
        else:
            src = rl.at[s, slot - 1, rows]
        return remote(src, rl.at[s, slot, rows], rs_send.at[s, slot, u], rs_recv.at[s, slot, u], (long_to, short_to)[way])

    def rs_wave(s, h, u):
        rows = pl.ds(u * SUB, SUB)
        for way in range(2):
            if h > 4 - way:
                continue
            rs_copy(s, way, h - 1, u).wait_recv()
            slot = h - 2 if way == 0 else 2 + h
            rl[s, slot, rows] = (rl[s, slot, rows].astype(F32) + yp[2 * (h - 1) + way, rows]).astype(BF16)
            rs_copy(s, way, h, u).start()

    def rs_last(s, u):
        rows = pl.ds(u * SUB, SUB)
        rs_copy(s, 1, 3, u).wait_recv()
        rs_copy(s, 0, 4, u).wait_recv()
        total = yp[7, rows] + rl[s, 3, rows].astype(F32) + rl[s, 6, rows].astype(F32)
        ef[s, c, z, rows] = (total - tv[s, rows].astype(F32)).astype(BF16)

    def rs_rest(s, work):
        for h in range(2, 5):
            for u in range(NSUB):
                rs_wave(s, h, u)
                run(work, (len(work) + NSUB * (5 - h) - u - 1) // (NSUB * (5 - h) - u))
        for u in range(NSUB):
            rs_last(s, u)
            if u < NSUB - 1:
                ag_wave(s, 1, u)

    def ag_copy(s, way, h, u):
        slot = h - 1 if way == 0 else 3 + h
        rows = pl.ds(u * SUB, SUB)
        origin = zz(-d * (h - 1)) if way == 0 else zz(d * (h - 1))
        block = ef.at[s, c, origin, rows]
        return remote(block, block, ag_send.at[s, slot, u], ag_recv.at[s, slot, u], (long_to, short_to)[way])

    def fw_copy(s, q):
        block = ef.at[s, c, zz(d * q)]
        k = q + 4 if q > -4 else 8
        return remote(block, block, fw_ssem.at[s, k], fw_rsem.at[s, k], partner)

    def fw_arrival(s, q):
        block = ef.at[s, o, zz(d * q)]
        k = 4 - q if q < 4 else 8
        return remote(block, block, fw_ssem.at[s, k], fw_rsem.at[s, k], partner)

    def ag_wave(s, h, u):
        for way in range(2):
            if h > 1 and h <= 5 - way:
                ag_copy(s, way, h - 1, u).wait_recv()
            if h <= 4 - way:
                ag_copy(s, way, h, u).start()
        if u == NSUB - 1:
            if h == 1:
                fw_copy(s, 0).start()
            else:
                fw_copy(s, 1 - h).start()
                if h <= 4:
                    fw_copy(s, h - 1).start()

    def ag_hop(s, h, work=(), low=0, high=NSUB):
        for u in range(low, high):
            ag_wave(s, h, u)
            run(work, (len(work) + high - u - 1) // (high - u))

    def arrange(s):
        pick = jnp.where(iota((NZ, 16), 1) == 2 * iota((NZ, 16), 0) + c, 1.0, 0.0).astype(BF16)
        half = n_rep * 8
        source = iota((half, lanes), 0)
        place = iota((half, lanes), 1)
        total = jnp.zeros((NZ, lanes), F32)
        for h in range(2):
            turned = lax.dot_general(
                pick, iv[h, s].astype(F32).astype(BF16), (((1,), (1,)), ((), ())), preferred_element_type=F32
            )
            to = jnp.where(place == (source // 8) * 16 + h * 8 + source % 8, 1.0, 0.0).astype(BF16)
            total += jnp.dot(turned.astype(BF16), to, preferred_element_type=F32)
        frow[s] = total

    def build_replicas(s, j):
        onehot = jnp.where(iota((BLOCK, lanes), 0).astype(F32) == frow[s, pl.ds(j, 1)], 1.0, 0.0).astype(BF16)
        kept = jnp.dot(bt[0], onehot, preferred_element_type=F32)
        for a in range(8):
            mine = (iota((BLOCK, lanes), 1) % 16) // 2 == a
            lu[s, j, a * BLOCK:(a + 1) * BLOCK] = jnp.where(mine, kept, 0.0).astype(BF16)

    def build_rows(s):
        lane = iota((lanes, BLOCK), 1)
        own = jnp.where(iota((lanes, BLOCK), 0) == 16 * r + lane % 16, 1.0, 0.0).astype(BF16)
        spread_rows = jnp.dot(frow[s].astype(BF16), own, preferred_element_type=F32)
        flat = jnp.where(iota((NZ, BLOCK), 1) // 16 == iota((NZ, BLOCK), 0), spread_rows, 0.0)
        row = jnp.sum(flat, axis=0, keepdims=True)
        onehot = jnp.where(iota((BLOCK, BLOCK), 0).astype(F32) == row, 1.0, 0.0).astype(BF16)
        kept = jnp.dot(bt[0], onehot, preferred_element_type=F32).T
        out = jnp.zeros((NZ * 16, TOK), F32)
        for h in range(2):
            for a in range(4):
                mine = (iota((BLOCK, BLOCK), 0) % 16) // 2 == 4 * h + a
                lx[:, a * BLOCK:(a + 1) * BLOCK] = jnp.where(mine, kept, 0.0).astype(BF16)
            out += lax.dot_general(lx[...], xa[s, h], (((1,), (1,)), ((), ())), preferred_element_type=F32)
        xr_send[s] = out.astype(BF16).reshape(NZ, 16, TOK)

    def xr_copy(s, k):
        to = zz(k)
        return remote(
            xr_send.at[s, to], xr_land.at[s, z], xr_ssem.at[s, k], xr_rsem.at[s, k], {"tp": 2 * to + c}
        )

    def rm_copy(s):
        return remote(rm_send.at[s, o], rm_land.at[s], rm_ssem.at[s], rm_rsem.at[s], partner)

    def kept_rows(s):
        for k in range(1, NZ):
            xr_copy(s, k).wait_recv()
        xr_land[s, z] = xr_send[s, z]
        table = xr_land[s].reshape(NZ * 16, TOK)
        out = jnp.dot(table, ef[s, c, z], preferred_element_type=F32) * (1.0 / TOK)
        s_send[s] = out.astype(BF16).reshape(NZ, 16, BLOCK)

    def sa_copy(s, k):
        to = zz(k)
        return remote(
            s_send.at[s, to], sn.at[s, c, z], sa_ssem.at[s, k], sa_rsem.at[s, k], {"tp": 2 * to + c}
        )

    def sp_copy(s):
        return remote(sn.at[s, c], sn.at[s, c], sp_ssem.at[s], sp_rsem.at[s], partner)

    parts_of = ((0, 2), (2, 5), (5, 8))

    def pl_copy(s, k, g):
        low, high = parts_of[g]
        return remote(
            ps.at[s, low:high], sall.at[s, r, low:high], pl_ssem.at[s, k, g], pl_rsem.at[s, k, g],
            {"rep": lax.rem(r + k, n_rep)},
        )

    def share(s):
        for k in range(1, NZ):
            sa_copy(s, k).start()
        sn[s, c, z] = s_send[s, z]

    def blend(s, g):
        for i in range(*parts_of[g]):
            j = zz(d * steps_out[i])
            own, other = rm_send[s, c, j], rm_land[s, j]
            rows = jnp.concatenate([jnp.where(c == 0, own, other), jnp.where(c == 0, other, own)], axis=0)
            total = (sn[s, c, j].astype(F32) + 0.9 * rows).astype(BF16)
            sn[s, c, j] = total
            ps[s, i] = total

    def spread(s, near):
        for k in (1, NZ - 1) if near else range(2, NZ - 1):
            sa_copy(s, k).wait_recv()
        if near:
            rm_copy(s).wait_recv()
        for g in (2,) if near else (0, 1):
            blend(s, g)
            for k in range(1, n_rep):
                pl_copy(s, k, g).start()
        if not near:
            sp_copy(s).start()
            sall[s, r] = ps[s]

    def collect(s, g):
        for k in range(1, n_rep):
            pl_copy(s, k, g).wait_recv()

    def update(s, i):
        j = zz(d * steps_out[i])
        stack = sall[s, :, i].reshape(lanes, BLOCK)
        for i in range(4):
            rows = pl.ds(i * 256, 256)
            change = jnp.dot(lu[s, j, rows], stack, preferred_element_type=F32)
            wb[j, rows] = (wb[j, rows].astype(F32) - 0.1 * change).astype(BF16)

    def momentum(s, q):
        fw_arrival(s, q).wait_recv()
        j = zz(d * q)
        e = jnp.concatenate([ef[s, 0, j], ef[s, 1, j]], axis=1)
        parts = []
        for h in range(2):
            both = sn[s, h, j].astype(F32)
            parts.append(jnp.where(c == 0, both[:8], both[8:]))
        zero = jnp.zeros((8, BLOCK), F32)
        top = jnp.concatenate([parts[0], zero], axis=1)
        low = jnp.concatenate([zero, parts[1]], axis=1)
        block = jnp.concatenate([top, top, low, low], axis=0)
        right = jnp.concatenate([jnp.where(j % 4 == i, block, 0.0) for i in range(4)], axis=0).astype(BF16)
        for i in range(2):
            rows = pl.ds(i * 256, 256)
            grad = jnp.dot(xt[s, rows], e, preferred_element_type=F32)
            taken = jnp.dot(left[s, j // 4, rows], right, preferred_element_type=F32)
            mb[j, rows] = 0.9 * mb[j, rows] + grad * (1.0 / TOK) - taken

    def gain(q):
        momentum(0, q)
        project(1, zz(d * q))

    def finish(q):
        momentum(1, q)
        j = zz(d * q)
        m_copy(j).start()

    def m_copy(j):
        columns = pl.ds(pl.multiple_of(2 * BLOCK * j, 2 * BLOCK), 2 * BLOCK)
        return pltpu.make_async_copy(mb.at[j], m_out.at[0, :, columns], out_sem.at[NZ + j])

    def run(work, count):
        for _ in range(min(count, len(work))):
            work.pop(0)()

    def turn(s):
        xt[s] = xa[s, c].T

    loads["x0"].wait()
    pairs[1].wait_recv()

    def ready(k):
        for i in (2 * k, 2 * k + 1):
            loads["w", i].wait()
            pairs[2 + i].wait_recv()

    ready(0)
    forward(0, 0)
    told(0, along_z)
    tell(1, two_on)
    ready(1)
    forward(0, 1)
    pairs[0].wait_recv()
    arrange(0)
    build_rows(0)
    ready(2)
    ready(3)
    told(1, two_on)
    for k in range(1, NZ):
        xr_copy(0, k).start()

    def pass_on(k, before, after):
        def act():
            told(k, before)
            tell(k + 1, after)

        return act

    def second_rows():
        loads["x1"].wait()
        pairs[10].wait_recv()
        arrange(1)
        build_rows(1)

    def two(f, s, j):
        return lambda: (f(s, j), f(s, j + 1))

    def products(first):
        def some():
            for j in (first, first + 1):
                loads["m", j].wait()
                project(0, j)

        return some

    rs_rest(0, [
        lambda: forward(0, 2),
        products(0),
        lambda: (products(2)(), pass_on(3, along_x, along_y)()),
        lambda: forward(0, 3),
        products(4),
        products(6),
        lambda: (rm_copy(0).start(), loads["t"].wait()),
        lambda: turn(0),
        second_rows,
        lambda: (two(build_replicas, 0, 0)(), pass_on(4, along_y, along_y)()),
        two(build_replicas, 0, 2),
        two(build_replicas, 0, 4),
        lambda: (two(build_replicas, 0, 6)(), told(5, along_y)),
    ])
    kept_rows(0)
    share(0)
    ag_wave(0, 1, NSUB - 1)
    spread(0, True)
    ag_hop(0, 2, (), 0, NSUB // 2)
    spread(0, False)
    ag_hop(0, 2, (), NSUB // 2, NSUB)
    for k in range(1, NZ):
        xr_copy(1, k).start()
    build_own(1, 0)
    build_own(1, 1)
    sp_copy(0).wait_recv()
    gain(0)
    ag_hop(0, 3)
    collect(0, 0)

    for k in range(4):
        if k == 1:
            collect(0, 1)
            collect(0, 2)
        update(0, 2 * k)
        update(0, 2 * k + 1)
        forward(1, k)
        if k == 1:
            ag_hop(0, 4)

    def last_gain():
        gain(4)
        rm_copy(1).start()

    rs_rest(1, [
        lambda: gain(1),
        lambda: gain(-1),
        lambda: gain(2),
        lambda: gain(-2),
        lambda: (ag_hop(0, 5), gain(3)),
        lambda: gain(-3),
        last_gain,
        lambda: turn(1),
        two(build_replicas, 1, 0),
        two(build_replicas, 1, 2),
        two(build_replicas, 1, 4),
        two(build_replicas, 1, 6),
    ])
    kept_rows(1)
    share(1)
    ag_wave(1, 1, NSUB - 1)
    spread(1, True)
    ag_hop(1, 2, (), 0, NSUB // 2)
    spread(1, False)
    ag_hop(1, 2, (), NSUB // 2, NSUB)
    sp_copy(1).wait_recv()
    ag_hop(1, 3, [lambda: finish(0), lambda: finish(1), lambda: finish(-1)])
    out_copies = []

    def new_weight(i):
        update(1, i)
        j = zz(d * steps_out[i])
        own = pltpu.make_async_copy(wb.at[j, half_own], w_out.at[:, cols(j, c)], out_sem.at[i])
        own.start()
        other = remote(wb.at[j, half_other], w_out.at[:, cols(j, c)], outp_ssem.at[i], outp_rsem.at[i], partner)
        other.start()
        out_copies.extend([own, other])

    ag_hop(1, 4, [lambda: finish(2), lambda: finish(-2)])
    for g in range(3):
        collect(1, g)
    for i in range(NZ):
        new_weight(i)
    ag_hop(1, 5, [lambda: finish(3), lambda: finish(-3)])
    finish(4)

    for copy in out_copies:
        copy.wait()
    for j in range(NZ):
        m_copy(j).wait()
    for copy in pairs:
        copy.wait_send()
    for s in range(STEPS):
        for way in range(2):
            for h in range(1, 5 - way):
                for u in range(NSUB):
                    rs_copy(s, way, h, u).wait_send()
                    ag_copy(s, way, h, u).wait_send()
        for q in range(-4, 4):
            fw_copy(s, q).wait_send()
        for k in range(1, NZ):
            xr_copy(s, k).wait_send()
            sa_copy(s, k).wait_send()
        rm_copy(s).wait_send()
        for k in range(1, n_rep):
            for g in range(3):
                pl_copy(s, k, g).wait_send()
        sp_copy(s).wait_send()


def local(n_rep, inputs, targets, weight, momentum, indices):
    lanes = n_rep * 16
    arranged = indices.transpose(0, 1, 2, 4, 3).reshape(STEPS, n_rep * 8, 2 * NZ)
    any_space = pl.BlockSpec(memory_space=pl.ANY)
    dma = pltpu.SemaphoreType.DMA
    scratch = [
        pltpu.VMEM((STEPS, 2, TOK, ROWS), BF16),
        pltpu.VMEM((STEPS, ROWS, TOK), BF16),
        pltpu.VMEM((STEPS, TOK, BLOCK), BF16),
        pltpu.VMEM((NZ, 2 * ROWS, BLOCK), BF16),
        pltpu.VMEM((NZ, ROWS, 2 * BLOCK), F32),
        pltpu.VMEM((2, STEPS, n_rep * 8, 2 * NZ), jnp.int32),
        pltpu.VMEM((2, BLOCK, BLOCK), BF16),
        pltpu.VMEM((STEPS, NZ, lanes), F32),
        pltpu.VMEM((STEPS, 2, ROWS, BLOCK), BF16),
        pltpu.VMEM((STEPS, NZ, 32, ROWS), BF16),
        pltpu.VMEM((STEPS, NZ, 2 * ROWS, lanes), BF16),
        pltpu.VMEM((NZ, TOK, BLOCK), F32),
        pltpu.VMEM((STEPS, 2, TOK, BLOCK), BF16),
        pltpu.VMEM((STEPS, 7, TOK, BLOCK), BF16),
        pltpu.VMEM((STEPS, 2, NZ, TOK, BLOCK), BF16),
        pltpu.VMEM((BLOCK, ROWS), BF16),
        pltpu.VMEM((STEPS, NZ, 16, TOK), BF16),
        pltpu.VMEM((STEPS, NZ, 16, TOK), BF16),
        pltpu.VMEM((STEPS, 2, NZ, 8, BLOCK), F32),
        pltpu.VMEM((STEPS, NZ, 8, BLOCK), F32),
        pltpu.VMEM((STEPS, NZ, 16, BLOCK), BF16),
        pltpu.VMEM((STEPS, 2, NZ, 16, BLOCK), BF16),
        pltpu.VMEM((STEPS, NZ, 16, BLOCK), BF16),
        pltpu.VMEM((STEPS, n_rep, NZ, 16, BLOCK), BF16),
        dma((24,)), dma((11,)), dma((11,)),
        dma((STEPS, 7, NSUB)), dma((STEPS, 7, NSUB)), dma((STEPS, 7, NSUB)), dma((STEPS, 7, NSUB)),
        dma((STEPS, NZ)), dma((STEPS, NZ)), dma((STEPS,)), dma((STEPS,)),
        dma((STEPS, NZ)), dma((STEPS, NZ)), dma((STEPS,)), dma((STEPS,)),
        dma((STEPS, n_rep, 3)), dma((STEPS, n_rep, 3)), dma((STEPS, NZ + 1)), dma((STEPS, NZ + 1)),
        dma((2 * NZ,)), dma((NZ,)), dma((NZ,)),
        pltpu.SemaphoreType.REGULAR((6,)),
    ]
    return pl.pallas_call(
        functools.partial(kernel, n_rep),
        out_shape=(
            jax.ShapeDtypeStruct(weight.shape, BF16),
            jax.ShapeDtypeStruct(momentum.shape, F32),
        ),
        in_specs=[pl.BlockSpec(memory_space=pltpu.HBM)] * 6,
        out_specs=(any_space, any_space),
        scratch_shapes=scratch,
        compiler_params=pltpu.CompilerParams(
            collective_id=0, has_side_effects=True, vmem_limit_bytes=40 << 20
        ),
    )(*[pltpu.with_memory_space_constraint(v, pltpu.HBM) for v in (inputs, targets, weight, momentum, arranged, jnp.asarray(basis_parts()))])


def solution(mesh):
    in_specs = (
        P(None, "rep", "tp"),
        P(None, "rep", "tp"),
        P("tp", None),
        P("rep", "tp", None),
        P(None, None, "tp", None, None),
    )
    out_specs = (P("tp", None), P("rep", "tp", None))
    return jax.shard_map(
        functools.partial(local, mesh.shape["rep"]), mesh=mesh, in_specs=in_specs, out_specs=out_specs, check_vma=False
    )
```

```python
import functools

import jax
import jax.numpy as jnp
import ml_dtypes
import numpy as np
from jax import lax
from jax.experimental import pallas as pl
from jax.experimental.pallas import tpu as pltpu
from jax.sharding import PartitionSpec as P

MESH = pl.DeviceIdType.MESH
BLOCK = 128
STEPS = 2
TOK = 512
NZ = 8
ROWS = 512
NSUB = 4
SIDE = 4
SUB = TOK // NSUB
F32 = jnp.float32
BF16 = jnp.bfloat16


def basis_parts():
    k = np.arange(BLOCK, dtype=np.float64)[:, None]
    n = np.arange(BLOCK, dtype=np.float64)[None, :]
    scale = np.where(k == 0, np.sqrt(1.0 / BLOCK), np.sqrt(2.0 / BLOCK))
    table = (scale * np.cos(np.pi * (2.0 * n + 1.0) * k / (2.0 * BLOCK))).T
    high = table.astype(ml_dtypes.bfloat16)
    low = (table - high.astype(np.float64)).astype(ml_dtypes.bfloat16)
    return np.stack([high, low])


def iota(shape, axis):
    return lax.broadcasted_iota(jnp.int32, shape, axis)


def kernel(
    n_rep,
    x_ref, t_ref, w_ref, m_ref, idx_ref, bt_ref,
    w_out, m_out,
    xa, xt, tv, wb, mb, iv, bt, frow, left, prow, lu,
    yp, ys, rl, ef, lx, xr_send, xr_land, rm_send, rm_land, s_send, sn, sall,
    load_sem, pair_send, pair_recv, rs_send, rs_recv, ag_send, ag_recv,
    xr_ssem, xr_rsem, rm_ssem, rm_rsem, sa_ssem, sa_rsem, sp_ssem, sp_rsem,
    pl_ssem, pl_rsem, fw_ssem, fw_rsem, out_sem, outp_ssem, outp_rsem, token,
):
    r = lax.axis_index("rep")
    me = lax.axis_index("tp")
    z = me // 2
    c = me % 2
    o = 1 - c
    lanes = n_rep * 16
    d = 1 - 2 * c
    partner = {"tp": 2 * z + o}

    def zz(k):
        return lax.rem(z + k + 2 * NZ, NZ)

    long_to = {"tp": 2 * zz(d) + c}
    short_to = {"tp": 2 * zz(-d) + c}

    def remote(src, dst, s, v, dev):
        return pltpu.make_async_remote_copy(
            src_ref=src, dst_ref=dst, send_sem=s, recv_sem=v, device_id=dev, device_id_type=MESH
        )

    def cols(j, h):
        return pl.ds(pl.multiple_of((2 * j + h) * BLOCK, BLOCK), BLOCK)

    half_own = pl.ds(pl.multiple_of(c * ROWS, ROWS), ROWS)
    half_other = pl.ds(pl.multiple_of(o * ROWS, ROWS), ROWS)

    side = SIDE
    along_x = [{"rep": (r // side) * side + lax.rem(r + k, side)} for k in (1, side - 1)]
    along_y = [{"rep": lax.rem(r + k * side, n_rep)} for k in (1, side - 1)]
    along_z = [long_to, short_to]
    two_on = [{"tp": 2 * zz(2) + c}, {"tp": 2 * zz(-2) + c}]
    if n_rep != side * side:
        along_x, along_y = [], []
    barrier = pltpu.get_barrier_semaphore()
    for peer in [partner] + along_z + along_x + along_y:
        pl.semaphore_signal(barrier, inc=1, device_id=peer, device_id_type=MESH)

    def tell(k, peers):
        for peer in peers:
            pl.semaphore_signal(token.at[k], inc=1, device_id=peer, device_id_type=MESH)

    def told(k, peers):
        if peers:
            pl.semaphore_wait(token.at[k], len(peers))

    loads = {}

    def load(name, k, src, dst):
        copy = pltpu.make_async_copy(src, dst, load_sem.at[k])
        copy.start()
        loads[name] = copy

    steps_out = (4, -3, 3, -2, 2, -1, 1, 0)
    load("ix", 2, idx_ref, iv.at[c])
    load("bt", 1, bt_ref, bt)
    load("x0", 0, x_ref.at[0], xa.at[0, c])
    for i in range(NZ):
        j = zz(d * steps_out[i])
        load(("w", i), 8 + i, w_ref.at[:, cols(j, c)], wb.at[j, half_own])
    load("x1", 3, x_ref.at[1], xa.at[1, c])
    load("t", 4, t_ref, tv)
    for j in range(NZ):
        load(("m", j), 16 + j, m_ref.at[0, :, pl.ds(2 * BLOCK * j, 2 * BLOCK)], mb.at[j])

    def build_own(s, g):
        mine = iv[c, s, pl.ds(pl.multiple_of(8 * r, 8), 8)].astype(F32).astype(BF16)
        lane = iota((16, BLOCK), 1)
        to = jnp.where(iota((16, BLOCK), 0) == 8 * g + lane // 16, 1.0, 0.0).astype(BF16)
        wide = jnp.dot(mine, to, preferred_element_type=F32)
        flat = jnp.where(iota((8, BLOCK), 1) % 8 == iota((8, BLOCK), 0), wide, 0.0)
        row = jnp.sum(flat, axis=0, keepdims=True)
        lane = iota((BLOCK, BLOCK), 1)
        hit = iota((BLOCK, BLOCK), 0).astype(F32) == row
        even = (lane // 8) % 2 == 0
        high = jnp.where(hit & even, 1.0, 0.0).astype(BF16)
        low = jnp.where(hit & jnp.logical_not(even), 1.0, 0.0).astype(BF16)
        both = jnp.dot(bt[0], high, preferred_element_type=F32) + jnp.dot(bt[1], low, preferred_element_type=F32)
        turned = both.T
        for a in range(4):
            left[s, g, a * BLOCK:(a + 1) * BLOCK] = jnp.where((lane % 8) // 2 == a, both, 0.0).astype(BF16)
            rows = jnp.where((iota((BLOCK, BLOCK), 0) % 8) // 2 == a, turned, 0.0).astype(BF16)
            prow[s, 4 * g:4 * g + 4, :, a * BLOCK:(a + 1) * BLOCK] = rows.reshape(4, 32, BLOCK)

    def project(s, j):
        table = prow[s, j]
        values = mb[j]
        high = values.astype(BF16)
        low = (values - high.astype(F32)).astype(BF16)
        out = jnp.dot(table, high, preferred_element_type=F32) + jnp.dot(table, low, preferred_element_type=F32)
        rm_send[s, 0, j] = out[0:8, :BLOCK] + out[8:16, :BLOCK]
        rm_send[s, 1, j] = out[16:24, BLOCK:] + out[24:32, BLOCK:]

    def early():
        loads["bt"].wait()
        loads["ix"].wait()
        build_own(0, 0)
        build_own(0, 1)

    early()
    pl.semaphore_wait(barrier, 1 + len(along_z + along_x + along_y))
    tell(0, along_z)
    tell(3, along_x)

    pairs = []

    def pair(k, src, dst):
        copy = remote(src, dst, pair_send.at[k], pair_recv.at[k], partner)
        copy.start()
        pairs.append(copy)

    pair(9, idx_ref, iv.at[c])
    pair(0, x_ref.at[0], xa.at[0, c])
    for i in range(NZ):
        j = zz(-d * steps_out[i])
        pair(1 + i, w_ref.at[:, cols(j, o)], wb.at[j, half_own])
    pair(10, x_ref.at[1], xa.at[1, c])

    order = [(zz(4 * d), zz(-3 * d)), (zz(3 * d), zz(-2 * d)), (zz(2 * d), zz(-d)), (zz(d), z)]

    def forward(s, k):
        p, q = order[k]
        for i in range(2):
            rows = pl.ds(i * 256, 256)
            acc = jnp.zeros((256, 2 * BLOCK), F32)
            for h in range(2):
                w = jnp.concatenate([wb[p, h * ROWS:(h + 1) * ROWS], wb[q, h * ROWS:(h + 1) * ROWS]], axis=1)
                acc += jnp.dot(xa[s, h, rows], w, preferred_element_type=F32)
            yp[2 * k, rows] = acc[:, :BLOCK]
            yp[2 * k + 1, rows] = acc[:, BLOCK:]
            if k == 0:
                ys[s, 0, rows] = acc[:, :BLOCK].astype(BF16)
                ys[s, 1, rows] = acc[:, BLOCK:].astype(BF16)
                for u in range(i * NSUB // 2, (i + 1) * NSUB // 2):
                    for way in range(2):
                        rs_copy(s, way, 1, u).start()

    def rs_copy(s, way, h, u):
        slot = h - 1 if way == 0 else 3 + h
        rows = pl.ds(u * SUB, SUB)
        if h == 1:
            src = ys.at[s, way, rows]
        else:
            src = rl.at[s, slot - 1, rows]
        return remote(src, rl.at[s, slot, rows], rs_send.at[s, slot, u], rs_recv.at[s, slot, u], (long_to, short_to)[way])

    def rs_wave(s, h, u):
        rows = pl.ds(u * SUB, SUB)
        for way in range(2):
            if h > 4 - way:
                continue
            rs_copy(s, way, h - 1, u).wait_recv()
            slot = h - 2 if way == 0 else 2 + h
            rl[s, slot, rows] = (rl[s, slot, rows].astype(F32) + yp[2 * (h - 1) + way, rows]).astype(BF16)
            rs_copy(s, way, h, u).start()

    def rs_last(s, u):
        rows = pl.ds(u * SUB, SUB)
        rs_copy(s, 1, 3, u).wait_recv()
        rs_copy(s, 0, 4, u).wait_recv()
        total = yp[7, rows] + rl[s, 3, rows].astype(F32) + rl[s, 6, rows].astype(F32)
        ef[s, c, z, rows] = (total - tv[s, rows].astype(F32)).astype(BF16)

    def rs_rest(s, work):
        for h in range(2, 5):
            for u in range(NSUB):
                rs_wave(s, h, u)
                run(work, (len(work) + NSUB * (5 - h) - u - 1) // (NSUB * (5 - h) - u))
        for u in range(NSUB):
            rs_last(s, u)
            if u < NSUB - 1:
                ag_wave(s, 1, u)

    def ag_copy(s, way, h, u):
        slot = h - 1 if way == 0 else 3 + h
        rows = pl.ds(u * SUB, SUB)
        origin = zz(-d * (h - 1)) if way == 0 else zz(d * (h - 1))
        block = ef.at[s, c, origin, rows]
        return remote(block, block, ag_send.at[s, slot, u], ag_recv.at[s, slot, u], (long_to, short_to)[way])

    def fw_copy(s, q):
        block = ef.at[s, c, zz(d * q)]
        k = q + 4 if q > -4 else 8
        return remote(block, block, fw_ssem.at[s, k], fw_rsem.at[s, k], partner)

    def fw_arrival(s, q):
        block = ef.at[s, o, zz(d * q)]
        k = 4 - q if q < 4 else 8
        return remote(block, block, fw_ssem.at[s, k], fw_rsem.at[s, k], partner)

    def ag_wave(s, h, u):
        for way in range(2):
            if h > 1 and h <= 5 - way:
                ag_copy(s, way, h - 1, u).wait_recv()
            if h <= 4 - way:
                ag_copy(s, way, h, u).start()
        if u == NSUB - 1:
            if h == 1:
                fw_copy(s, 0).start()
            else:
                fw_copy(s, 1 - h).start()
                if h <= 4:
                    fw_copy(s, h - 1).start()

    def ag_hop(s, h, work=(), low=0, high=NSUB):
        for u in range(low, high):
            ag_wave(s, h, u)
            run(work, (len(work) + high - u - 1) // (high - u))

    def arrange(s):
        pick = jnp.where(iota((NZ, 16), 1) == 2 * iota((NZ, 16), 0) + c, 1.0, 0.0).astype(BF16)
        half = n_rep * 8
        source = iota((half, lanes), 0)
        place = iota((half, lanes), 1)
        total = jnp.zeros((NZ, lanes), F32)
        for h in range(2):
            turned = lax.dot_general(
                pick, iv[h, s].astype(F32).astype(BF16), (((1,), (1,)), ((), ())), preferred_element_type=F32
            )
            to = jnp.where(place == (source // 8) * 16 + h * 8 + source % 8, 1.0, 0.0).astype(BF16)
            total += jnp.dot(turned.astype(BF16), to, preferred_element_type=F32)
        frow[s] = total

    def build_replicas(s, j):
        onehot = jnp.where(iota((BLOCK, lanes), 0).astype(F32) == frow[s, pl.ds(j, 1)], 1.0, 0.0).astype(BF16)
        kept = jnp.dot(bt[0], onehot, preferred_element_type=F32)
        for a in range(8):
            mine = (iota((BLOCK, lanes), 1) % 16) // 2 == a
            lu[s, j, a * BLOCK:(a + 1) * BLOCK] = jnp.where(mine, kept, 0.0).astype(BF16)

    def build_rows(s):
        lane = iota((lanes, BLOCK), 1)
        own = jnp.where(iota((lanes, BLOCK), 0) == 16 * r + lane % 16, 1.0, 0.0).astype(BF16)
        spread_rows = jnp.dot(frow[s].astype(BF16), own, preferred_element_type=F32)
        flat = jnp.where(iota((NZ, BLOCK), 1) // 16 == iota((NZ, BLOCK), 0), spread_rows, 0.0)
        row = jnp.sum(flat, axis=0, keepdims=True)
        onehot = jnp.where(iota((BLOCK, BLOCK), 0).astype(F32) == row, 1.0, 0.0).astype(BF16)
        kept = jnp.dot(bt[0], onehot, preferred_element_type=F32).T
        out = jnp.zeros((NZ * 16, TOK), F32)
        for h in range(2):
            for a in range(4):
                mine = (iota((BLOCK, BLOCK), 0) % 16) // 2 == 4 * h + a
                lx[:, a * BLOCK:(a + 1) * BLOCK] = jnp.where(mine, kept, 0.0).astype(BF16)
            out += lax.dot_general(lx[...], xa[s, h], (((1,), (1,)), ((), ())), preferred_element_type=F32)
        xr_send[s] = out.astype(BF16).reshape(NZ, 16, TOK)

    def xr_copy(s, k):
        to = zz(k)
        return remote(
            xr_send.at[s, to], xr_land.at[s, z], xr_ssem.at[s, k], xr_rsem.at[s, k], {"tp": 2 * to + c}
        )

    def rm_copy(s):
        return remote(rm_send.at[s, o], rm_land.at[s], rm_ssem.at[s], rm_rsem.at[s], partner)

    def kept_rows(s):
        for k in range(1, NZ):
            xr_copy(s, k).wait_recv()
        xr_land[s, z] = xr_send[s, z]
        table = xr_land[s].reshape(NZ * 16, TOK)
        out = jnp.dot(table, ef[s, c, z], preferred_element_type=F32) * (1.0 / TOK)
        s_send[s] = out.astype(BF16).reshape(NZ, 16, BLOCK)

    def sa_copy(s, k):
        to = zz(k)
        return remote(
            s_send.at[s, to], sn.at[s, c, z], sa_ssem.at[s, k], sa_rsem.at[s, k], {"tp": 2 * to + c}
        )

    def sp_copy(s):
        return remote(sn.at[s, c], sn.at[s, c], sp_ssem.at[s], sp_rsem.at[s], partner)

    def pl_copy(s, k):
        return remote(
            sn.at[s, c], sall.at[s, r], pl_ssem.at[s, k], pl_rsem.at[s, k], {"rep": lax.rem(r + k, n_rep)}
        )

    def share(s):
        for k in range(1, NZ):
            sa_copy(s, k).start()
        sn[s, c, z] = s_send[s, z]

    def spread(s):
        for k in range(1, NZ):
            sa_copy(s, k).wait_recv()
        rm_copy(s).wait_recv()
        own, other = rm_send[s, c], rm_land[s]
        rows = jnp.concatenate([jnp.where(c == 0, own, other), jnp.where(c == 0, other, own)], axis=1)
        sn[s, c] = (sn[s, c].astype(F32) + 0.9 * rows).astype(BF16)
        for k in range(1, n_rep):
            pl_copy(s, k).start()
        sp_copy(s).start()
        sall[s, r] = sn[s, c]

    def collect(s):
        for k in range(1, n_rep):
            pl_copy(s, k).wait_recv()

    def update(s, j):
        stack = sall[s, :, j].reshape(lanes, BLOCK)
        for i in range(4):
            rows = pl.ds(i * 256, 256)
            change = jnp.dot(lu[s, j, rows], stack, preferred_element_type=F32)
            wb[j, rows] = (wb[j, rows].astype(F32) - 0.1 * change).astype(BF16)

    def momentum(s, q):
        fw_arrival(s, q).wait_recv()
        j = zz(d * q)
        e = jnp.concatenate([ef[s, 0, j], ef[s, 1, j]], axis=1)
        parts = []
        for h in range(2):
            both = sn[s, h, j].astype(F32)
            parts.append(jnp.where(c == 0, both[:8], both[8:]))
        zero = jnp.zeros((8, BLOCK), F32)
        top = jnp.concatenate([parts[0], zero], axis=1)
        low = jnp.concatenate([zero, parts[1]], axis=1)
        block = jnp.concatenate([top, top, low, low], axis=0)
        right = jnp.concatenate([jnp.where(j % 4 == i, block, 0.0) for i in range(4)], axis=0).astype(BF16)
        for i in range(2):
            rows = pl.ds(i * 256, 256)
            grad = jnp.dot(xt[s, rows], e, preferred_element_type=F32)
            taken = jnp.dot(left[s, j // 4, rows], right, preferred_element_type=F32)
            mb[j, rows] = 0.9 * mb[j, rows] + grad * (1.0 / TOK) - taken

    def gain(q):
        momentum(0, q)
        project(1, zz(d * q))

    def finish(q):
        momentum(1, q)
        j = zz(d * q)
        m_copy(j).start()

    def m_copy(j):
        columns = pl.ds(pl.multiple_of(2 * BLOCK * j, 2 * BLOCK), 2 * BLOCK)
        return pltpu.make_async_copy(mb.at[j], m_out.at[0, :, columns], out_sem.at[NZ + j])

    def run(work, count):
        for _ in range(min(count, len(work))):
            work.pop(0)()

    def turn(s):
        xt[s] = xa[s, c].T

    loads["x0"].wait()
    pairs[1].wait_recv()

    def ready(k):
        for i in (2 * k, 2 * k + 1):
            loads["w", i].wait()
            pairs[2 + i].wait_recv()

    ready(0)
    forward(0, 0)
    told(0, along_z)
    tell(1, two_on)
    ready(1)
    forward(0, 1)
    pairs[0].wait_recv()
    arrange(0)
    build_rows(0)
    ready(2)
    ready(3)
    told(1, two_on)
    for k in range(1, NZ):
        xr_copy(0, k).start()

    def pass_on(k, before, after):
        def act():
            told(k, before)
            tell(k + 1, after)

        return act

    def second_rows():
        loads["x1"].wait()
        pairs[10].wait_recv()
        arrange(1)
        build_rows(1)

    def two(f, s, j):
        return lambda: (f(s, j), f(s, j + 1))

    def products(first):
        def some():
            for j in (first, first + 1):
                loads["m", j].wait()
                project(0, j)

        return some

    rs_rest(0, [
        lambda: forward(0, 2),
        products(0),
        lambda: (products(2)(), pass_on(3, along_x, along_y)()),
        lambda: forward(0, 3),
        products(4),
        products(6),
        lambda: (rm_copy(0).start(), loads["t"].wait()),
        lambda: turn(0),
        second_rows,
        lambda: (two(build_replicas, 0, 0)(), pass_on(4, along_y, along_y)()),
        two(build_replicas, 0, 2),
        two(build_replicas, 0, 4),
        lambda: (two(build_replicas, 0, 6)(), told(5, along_y)),
    ])
    kept_rows(0)
    share(0)
    ag_wave(0, 1, NSUB - 1)
    ag_hop(0, 2, (), 0, NSUB // 2)
    spread(0)
    ag_hop(0, 2, (), NSUB // 2, NSUB)
    build_own(1, 0)
    build_own(1, 1)
    ag_hop(0, 3)
    for k in range(1, NZ):
        xr_copy(1, k).start()
    sp_copy(0).wait_recv()
    gain(0)
    gain(1)
    gain(-1)
    ag_hop(0, 4)
    collect(0)

    for k in range(4):
        update(0, order[k][0])
        update(0, order[k][1])
        forward(1, k)

    def last_gain():
        gain(4)
        rm_copy(1).start()

    rs_rest(1, [
        lambda: gain(2),
        lambda: gain(-2),
        lambda: (ag_hop(0, 5), gain(3)),
        lambda: gain(-3),
        last_gain,
        lambda: turn(1),
        two(build_replicas, 1, 0),
        two(build_replicas, 1, 2),
        two(build_replicas, 1, 4),
        two(build_replicas, 1, 6),
    ])
    kept_rows(1)
    share(1)
    ag_wave(1, 1, NSUB - 1)
    ag_hop(1, 2, (), 0, NSUB // 2)
    spread(1)
    ag_hop(1, 2, (), NSUB // 2, NSUB)
    sp_copy(1).wait_recv()
    ag_hop(1, 3, [lambda: finish(0), lambda: finish(1), lambda: finish(-1)])
    out_copies = []

    def new_weight(j):
        update(1, j)
        own = pltpu.make_async_copy(wb.at[j, half_own], w_out.at[:, cols(j, c)], out_sem.at[j])
        own.start()
        other = remote(wb.at[j, half_other], w_out.at[:, cols(j, c)], outp_ssem.at[j], outp_rsem.at[j], partner)
        other.start()
        out_copies.extend([own, other])

    ag_hop(1, 4, [lambda: finish(2), lambda: finish(-2)])
    collect(1)
    for j in range(NZ):
        new_weight(j)
    ag_hop(1, 5, [lambda: finish(3), lambda: finish(-3)])
    finish(4)

    for copy in out_copies:
        copy.wait()
    for j in range(NZ):
        m_copy(j).wait()
    for copy in pairs:
        copy.wait_send()
    for s in range(STEPS):
        for way in range(2):
            for h in range(1, 5 - way):
                for u in range(NSUB):
                    rs_copy(s, way, h, u).wait_send()
                    ag_copy(s, way, h, u).wait_send()
        for q in range(-4, 4):
            fw_copy(s, q).wait_send()
        for k in range(1, NZ):
            xr_copy(s, k).wait_send()
            sa_copy(s, k).wait_send()
        rm_copy(s).wait_send()
        for k in range(1, n_rep):
            pl_copy(s, k).wait_send()
        sp_copy(s).wait_send()


def settle(w_ref, m_ref, w_out, m_out, sem):
    copies = []
    for k in range(8):
        rows = pl.ds(k * 64, 64)
        copies.append(pltpu.make_async_copy(m_ref.at[0, rows], m_out.at[0, rows], sem.at[k]))
    for k in range(4):
        rows = pl.ds(k * 128, 128)
        copies.append(pltpu.make_async_copy(w_ref.at[rows], w_out.at[rows], sem.at[8 + k]))
    for copy in copies:
        copy.start()
    for copy in copies:
        copy.wait()


def local(n_rep, inputs, targets, weight, momentum, indices):
    lanes = n_rep * 16
    arranged = indices.transpose(0, 1, 2, 4, 3).reshape(STEPS, n_rep * 8, 2 * NZ)
    any_space = pl.BlockSpec(memory_space=pl.ANY)
    dma = pltpu.SemaphoreType.DMA
    scratch = [
        pltpu.VMEM((STEPS, 2, TOK, ROWS), BF16),
        pltpu.VMEM((STEPS, ROWS, TOK), BF16),
        pltpu.VMEM((STEPS, TOK, BLOCK), BF16),
        pltpu.VMEM((NZ, 2 * ROWS, BLOCK), BF16),
        pltpu.VMEM((NZ, ROWS, 2 * BLOCK), F32),
        pltpu.VMEM((2, STEPS, n_rep * 8, 2 * NZ), jnp.int32),
        pltpu.VMEM((2, BLOCK, BLOCK), BF16),
        pltpu.VMEM((STEPS, NZ, lanes), F32),
        pltpu.VMEM((STEPS, 2, ROWS, BLOCK), BF16),
        pltpu.VMEM((STEPS, NZ, 32, ROWS), BF16),
        pltpu.VMEM((STEPS, NZ, 2 * ROWS, lanes), BF16),
        pltpu.VMEM((NZ, TOK, BLOCK), F32),
        pltpu.VMEM((STEPS, 2, TOK, BLOCK), BF16),
        pltpu.VMEM((STEPS, 7, TOK, BLOCK), BF16),
        pltpu.VMEM((STEPS, 2, NZ, TOK, BLOCK), BF16),
        pltpu.VMEM((BLOCK, ROWS), BF16),
        pltpu.VMEM((STEPS, NZ, 16, TOK), BF16),
        pltpu.VMEM((STEPS, NZ, 16, TOK), BF16),
        pltpu.VMEM((STEPS, 2, NZ, 8, BLOCK), F32),
        pltpu.VMEM((STEPS, NZ, 8, BLOCK), F32),
        pltpu.VMEM((STEPS, NZ, 16, BLOCK), BF16),
        pltpu.VMEM((STEPS, 2, NZ, 16, BLOCK), BF16),
        pltpu.VMEM((STEPS, n_rep, NZ, 16, BLOCK), BF16),
        dma((24,)), dma((11,)), dma((11,)),
        dma((STEPS, 7, NSUB)), dma((STEPS, 7, NSUB)), dma((STEPS, 7, NSUB)), dma((STEPS, 7, NSUB)),
        dma((STEPS, NZ)), dma((STEPS, NZ)), dma((STEPS,)), dma((STEPS,)),
        dma((STEPS, NZ)), dma((STEPS, NZ)), dma((STEPS,)), dma((STEPS,)),
        dma((STEPS, n_rep)), dma((STEPS, n_rep)), dma((STEPS, NZ + 1)), dma((STEPS, NZ + 1)),
        dma((2 * NZ,)), dma((NZ,)), dma((NZ,)),
        pltpu.SemaphoreType.REGULAR((6,)),
    ]
    new_weight, new_momentum = pl.pallas_call(
        functools.partial(kernel, n_rep),
        out_shape=(
            jax.ShapeDtypeStruct(weight.shape, BF16),
            jax.ShapeDtypeStruct(momentum.shape, F32),
        ),
        in_specs=[pl.BlockSpec(memory_space=pltpu.HBM)] * 6,
        out_specs=(any_space, any_space),
        scratch_shapes=scratch,
        compiler_params=pltpu.CompilerParams(
            collective_id=0, has_side_effects=True, vmem_limit_bytes=40 << 20
        ),
    )(*[pltpu.with_memory_space_constraint(v, pltpu.HBM) for v in (inputs, targets, weight, momentum, arranged, jnp.asarray(basis_parts()))])
    return pl.pallas_call(
        settle,
        out_shape=(
            jax.ShapeDtypeStruct(weight.shape, BF16),
            jax.ShapeDtypeStruct(momentum.shape, F32),
        ),
        in_specs=[any_space] * 2,
        out_specs=(pl.BlockSpec(memory_space=pltpu.HBM),) * 2,
        scratch_shapes=[dma((12,))],
        compiler_params=pltpu.CompilerParams(vmem_limit_bytes=1 << 20),
    )(new_weight, new_momentum)


def solution(mesh):
    in_specs = (
        P(None, "rep", "tp"),
        P(None, "rep", "tp"),
        P("tp", None),
        P("rep", "tp", None),
        P(None, None, "tp", None, None),
    )
    out_specs = (P("tp", None), P("rep", "tp", None))
    return jax.shard_map(
        functools.partial(local, mesh.shape["rep"]), mesh=mesh, in_specs=in_specs, out_specs=out_specs, check_vma=False
    )
```
